32 devices in a mesh: face: 4 (over y, x), tile: 8 (over z, core).
Axes of the slice: x: 2, y: 2, z: 4, core: 2. Of those that a mesh axis runs over, the one named last changes fastest.
Arguments:
- state_field: bfloat16 [4, 256, 512, 256], P(None, 'face', 'tile'), may hold values from -6 to 6
- cotangent: bfloat16 [4, 256, 512, 256], P(None, 'face', 'tile'), may hold values from -6 to 6
- depth_weight: float32 [9, 256], replicated, may hold values from -2 to 2
- depth_bias: float32 [256], replicated, may hold values from -3 to 3
- point_weight: bfloat16 [256, 256], replicated, may hold values from -0.375 to 0.375
- tile_links: int32 [32, 4], P(('face', 'tile')), may hold values from 0 to 31, as said below
- link_sides: int32 [32, 4], P(('face', 'tile')), may hold values from 0 to 3
- link_flips: int32 [32, 4], P(('face', 'tile')), may hold values from 0 to 1
- corner_masks: int32 [32, 4], P(('face', 'tile')), may hold values 0 or 1
Outputs:
- field_grad: bfloat16 [4, 256, 512, 256], P(None, 'face', 'tile')
- depth_grad: float32 [9, 256], replicated
- bias_grad: float32 [256], replicated
- point_grad: float32 [256, 256], replicated
The draws below stay inside these ranges and needn't reach their ends.
Inputs may be any that keep to these rules, and one draw needn't show every extreme that they name: Tile ids number the grid row by row, the row being the index along face. The four neighbours of a tile are the four tiles one step away along face or along tile with wrap-around, each exactly once. Links are mutual: if tile_links[a, s] = b and link_sides[a, s] = o then tile_links[b, o] = a, link_sides[b, o] = s and link_flips[b, o] = link_flips[a, s].
All inputs are finite; a program needn't handle non-finite values. No bound on the sum of `corner_masks` on one device may be relied on, other than what follows from the above.
Results may differ from the reference program's by a relative error of at most 0.0049.
Values may be sent and summed in bfloat16 or wider, within the bound.
A program may use at most 192 MiB of HBM per device.

```python
import jax
import jax.numpy as jnp
from jax import lax

CH = 256
BATCH = 4
SIDE = 64
TILES = 32
PIXELS = 524288
N_FACE = 4
N_TILE = 8


def tile_graph(key):
    rotation = jax.random.randint(jax.random.fold_in(key, 11), (N_FACE, N_TILE), 0, 4)
    flip_south = jax.random.randint(jax.random.fold_in(key, 12), (N_FACE, N_TILE), 0, 2)
    flip_east = jax.random.randint(jax.random.fold_in(key, 13), (N_FACE, N_TILE), 0, 2)
    face_rows = jnp.arange(N_FACE, dtype=jnp.int32)[:, None, None]
    tile_cols = jnp.arange(N_TILE, dtype=jnp.int32)[None, :, None]
    side_ids = jnp.arange(4, dtype=jnp.int32)[None, None, :]
    heading = (side_ids + rotation[:, :, None]) % 4
    step_face = jnp.where(heading == 0, -1, jnp.where(heading == 2, 1, 0))
    step_tile = jnp.where(heading == 1, 1, jnp.where(heading == 3, -1, 0))
    other_face = (face_rows + step_face) % N_FACE
    other_tile = (tile_cols + step_tile) % N_TILE
    linked = other_face * N_TILE + other_tile
    facing = (heading + 2 - rotation[other_face, other_tile]) % 4
    own_south = jnp.broadcast_to(flip_south[:, :, None], heading.shape)
    own_east = jnp.broadcast_to(flip_east[:, :, None], heading.shape)
    far_south = flip_south[other_face, other_tile]
    far_east = flip_east[other_face, other_tile]
    flipping = jnp.where(heading == 2, own_south, jnp.where(heading == 1, own_east, jnp.where(heading == 0, far_south, far_east)))
    return (linked.reshape(TILES, 4).astype(jnp.int32), facing.reshape(TILES, 4).astype(jnp.int32), flipping.reshape(TILES, 4).astype(jnp.int32))


def draw_tile_links(key, part):
    return tile_graph(key)[0]


def draw_link_sides(key, part):
    return tile_graph(key)[1]


def draw_link_flips(key, part):
    return tile_graph(key)[2]


def with_ends(drawn, own_key, least, high):
    shape = drawn.shape
    place = [jax.random.randint(jax.random.fold_in(own_key, axis), (), 0, shape[axis]) for axis in range(len(shape))]
    drawn = drawn.at[tuple(place)].set(least)
    longest = shape.index(max(shape))
    place[longest] = (place[longest] + 1) % shape[longest]
    return drawn.at[tuple(place)].set(high)


def steps_of(rng, extent, cuts, smallest, top_value):
    loudness, own = 1.0, jax.random.fold_in(rng, 6)
    for axis_at, shards_of in cuts:
        steps = jnp.exp(jax.random.uniform(jax.random.fold_in(own, axis_at), (shards_of,), jnp.float32, smallest / len(cuts), top_value / len(cuts)))
        loudness = loudness * jnp.repeat(steps, extent[axis_at] // shards_of).reshape([-1 if axis == axis_at else 1 for axis in range(len(extent))])
    return loudness


def bell_draw(stream_key, dims, scale, bound, shards=(), held_as=jnp.bfloat16):
    gain = steps_of(stream_key, dims, shards, -0.22, 0.18) if shards else 1.0
    drawn = jax.random.normal(stream_key, dims, jnp.float32) * scale * gain
    return jnp.minimum(jnp.maximum(drawn, -bound), bound).astype(held_as)


def setup_inputs(seed: int = 0) -> dict:
    splits = jax.random.split(jax.random.key(seed), 10)
    state_field = bell_draw(splits[0], (BATCH, N_FACE * SIDE, N_TILE * SIDE, CH), 1.0, 6.0, ((1, 4), (2, 8)))
    cotangent = bell_draw(splits[1], (BATCH, N_FACE * SIDE, N_TILE * SIDE, CH), 1.0, 6.0, ((1, 4), (2, 8)))
    depth_weight = bell_draw(splits[2], (9, CH), 9 ** -0.5, 2.0, (), jnp.float32)
    depth_bias = bell_draw(splits[3], (CH,), 0.5, 3.0, (), jnp.float32)
    point_weight = bell_draw(splits[4], (CH, CH), CH ** -0.5, 0.375)
    tile_links = draw_tile_links(jax.random.fold_in(splits[9], 71), 0)
    link_sides = draw_link_sides(jax.random.fold_in(splits[9], 71), 0)
    link_flips = draw_link_flips(jax.random.fold_in(splits[9], 71), 0)
    corner_masks = with_ends((jax.random.randint(splits[8], (TILES, 4), 0, 4) < 3).astype(jnp.int32), jax.random.fold_in(splits[8], 1), 0, 1)
    return {"state_field": state_field, "cotangent": cotangent, "depth_weight": depth_weight, "depth_bias": depth_bias, "point_weight": point_weight, "tile_links": tile_links, "link_sides": link_sides, "link_flips": link_flips, "corner_masks": corner_masks}


root_two_pi = 0.7978845608028654
cubic_coef = 0.044715


def gelu_pair(hidden):
    inside = root_two_pi * (hidden + cubic_coef * hidden * hidden * hidden)
    tanh_val = jnp.tanh(inside)
    output = 0.5 * hidden * (1.0 + tanh_val)
    slope = 0.5 * (1.0 + tanh_val) + 0.5 * hidden * (1.0 - tanh_val * tanh_val) * root_two_pi * (1.0 + 3.0 * cubic_coef * hidden * hidden)
    return output, slope


def edge_rows(block):
    return jnp.stack([block[:, 0], block[:, :, -1], block[:, -1], block[:, :, 0]], axis=0)


def padded_tile(block, rim_rows, corner_row):
    cmask = corner_row.astype(jnp.float32)
    rim32 = rim_rows.astype(jnp.float32)
    north_west = (cmask[0] * 0.5 * (rim32[0][:, 0] + rim32[3][:, 0])).astype(jnp.bfloat16)
    north_east = (cmask[1] * 0.5 * (rim32[0][:, -1] + rim32[1][:, 0])).astype(jnp.bfloat16)
    south_east = (cmask[2] * 0.5 * (rim32[1][:, -1] + rim32[2][:, -1])).astype(jnp.bfloat16)
    south_west = (cmask[3] * 0.5 * (rim32[2][:, 0] + rim32[3][:, -1])).astype(jnp.bfloat16)
    top_row = jnp.concatenate([north_west[:, None], rim_rows[0], north_east[:, None]], axis=1)
    low_row = jnp.concatenate([south_west[:, None], rim_rows[2], south_east[:, None]], axis=1)
    middle = jnp.concatenate([rim_rows[3][:, :, None], block, rim_rows[1][:, :, None]], axis=2)
    return jnp.concatenate([top_row[:, None], middle, low_row[:, None]], axis=1)


def tile_pass(block, cotan, rim_rows, corner_row, depth_weight, depth_bias, point_weight):
    tile_side = block.shape[1]
    channels = block.shape[3]
    padded = padded_tile(block, rim_rows, corner_row)
    tap_table = depth_weight.reshape(3, 3, channels)
    hidden = jnp.zeros(block.shape, jnp.float32) + depth_bias
    for row_off in range(3):
        for col_off in range(3):
            hidden = hidden + tap_table[row_off, col_off] * padded[:, row_off:row_off + tile_side, col_off:col_off + tile_side].astype(jnp.float32)
    output, slope = gelu_pair(hidden)
    act = output.astype(jnp.bfloat16)
    row_count = block.shape[0] * tile_side * tile_side
    cot_rows = cotan.reshape(row_count, channels)
    grad_act = jnp.dot(cot_rows, point_weight.T, preferred_element_type=jnp.float32)
    grad_hidden = (grad_act.reshape(hidden.shape) * slope).astype(jnp.bfloat16)
    point_part = jnp.dot(act.reshape(row_count, channels).T, cot_rows, preferred_element_type=jnp.float32)
    grad32 = grad_hidden.astype(jnp.float32)
    depth_list = []
    grad_pad = jnp.zeros(padded.shape, jnp.float32)
    for row_off in range(3):
        for col_off in range(3):
            window = padded[:, row_off:row_off + tile_side, col_off:col_off + tile_side].astype(jnp.float32)
            depth_list.append(jnp.sum(grad32 * window, axis=(0, 1, 2)))
            grad_pad = grad_pad.at[:, row_off:row_off + tile_side, col_off:col_off + tile_side].add(tap_table[row_off, col_off] * grad32)
    depth_part = jnp.stack(depth_list, axis=0)
    bias_part = jnp.sum(grad32, axis=(0, 1, 2))
    inner_grad = grad_pad[:, 1:-1, 1:-1]
    cmask = corner_row.astype(jnp.float32)
    north_west = 0.5 * cmask[0] * grad_pad[:, 0, 0]
    north_east = 0.5 * cmask[1] * grad_pad[:, 0, -1]
    south_east = 0.5 * cmask[2] * grad_pad[:, -1, -1]
    south_west = 0.5 * cmask[3] * grad_pad[:, -1, 0]
    north = grad_pad[:, 0, 1:-1].at[:, 0].add(north_west).at[:, -1].add(north_east)
    east = grad_pad[:, 1:-1, -1].at[:, 0].add(north_east).at[:, -1].add(south_east)
    south = grad_pad[:, -1, 1:-1].at[:, 0].add(south_west).at[:, -1].add(south_east)
    west = grad_pad[:, 1:-1, 0].at[:, 0].add(north_west).at[:, -1].add(south_west)
    rim_grad = jnp.stack([north, east, south, west], axis=0)
    return rim_grad, point_part, depth_part, bias_part, inner_grad


def reference(state_field, cotangent, depth_weight, depth_bias, point_weight, tile_links, link_sides, link_flips, corner_masks):
    def to_tiles(whole):
        return whole.reshape(BATCH, N_FACE, SIDE, N_TILE, SIDE, CH).transpose(1, 3, 0, 2, 4, 5).reshape(TILES, BATCH, SIDE, SIDE, CH)

    tiles = to_tiles(state_field)
    cot_tiles = to_tiles(cotangent)
    edges = jax.vmap(edge_rows)(tiles)
    sources = edges[tile_links, link_sides]
    flipped = (link_flips == 1)[:, :, None, None, None]
    rim_all = jnp.where(flipped, sources[:, :, :, ::-1], sources)

    def first_pass(items):
        outcome = tile_pass(items[0], items[1], items[2], items[3], depth_weight, depth_bias, point_weight)
        return outcome[0], outcome[1], outcome[2], outcome[3]

    rim_grads, point_parts, depth_parts, bias_parts = lax.map(first_pass, (tiles, cot_tiles, rim_all, corner_masks))
    incoming = rim_grads[tile_links, link_sides]
    incoming = jnp.where(flipped, incoming[:, :, :, ::-1], incoming)

    def second_pass(items):
        inner_grad = tile_pass(items[0], items[1], items[2], items[3], depth_weight, depth_bias, point_weight)[4]
        extra = items[4]
        inner_grad = inner_grad.at[:, 0].add(extra[0]).at[:, :, -1].add(extra[1]).at[:, -1].add(extra[2]).at[:, :, 0].add(extra[3])
        return inner_grad.astype(jnp.bfloat16)

    grad_tiles = lax.map(second_pass, (tiles, cot_tiles, rim_all, corner_masks, incoming))
    field_grad = grad_tiles.reshape(N_FACE, N_TILE, BATCH, SIDE, SIDE, CH).transpose(2, 0, 3, 1, 4, 5).reshape(BATCH, N_FACE * SIDE, N_TILE * SIDE, CH)
    norm_scale = float(PIXELS) ** -0.5
    depth_grad = jnp.sum(depth_parts, axis=0) * norm_scale
    bias_grad = jnp.sum(bias_parts, axis=0) * norm_scale
    point_grad = jnp.sum(point_parts, axis=0) * norm_scale
    return field_grad, depth_grad, bias_grad, point_grad
```

```python
import functools

import jax
import jax.numpy as jnp
from jax import lax
from jax.experimental import pallas as pl
from jax.experimental.pallas import tpu as pltpu
from jax.sharding import PartitionSpec as P

root_two_pi = 0.7978845608028654
cubic_coef = 0.044715
HALF = 128
STRIP = 16
ROWS = 16
F32 = jnp.float32
BF16 = jnp.bfloat16


def gelu_pair(hidden):
    square = hidden * hidden
    gate = 0.5 + 0.5 * jnp.tanh(hidden * (root_two_pi + (root_two_pi * cubic_coef) * square))
    output = hidden * gate
    slope = gate + output * (1.0 - gate) * (
        2.0 * root_two_pi + (6.0 * root_two_pi * cubic_coef) * square
    )
    return output, slope


def first_kernel(
    norm_scale,
    x_ref,
    cot_ref,
    ends_ref,
    west_ref,
    east_ref,
    taps_ref,
    bias_ref,
    point_ref,
    g_ref,
    gwest_ref,
    geast_ref,
    sums_ref,
    win,
    grad_act,
    act,
    parts,
):
    sample, step = pl.program_id(0), pl.program_id(1)
    side, channels = x_ref.shape[1], x_ref.shape[3]
    rows = cot_ref.shape[1]

    @pl.when(step == 0)
    def _():
        for col_off in range(3):
            win[col_off, 0] = ends_ref[0, 0, col_off].astype(F32)
            win[col_off, side + 1] = ends_ref[0, 1, col_off].astype(F32)
        spot = lax.broadcasted_iota(jnp.int32, (side, HALF), 0)
        for lane in range(0, channels, HALF):
            lanes = pl.ds(lane, HALF)

            def shift(i, carry):
                mid = x_ref[0, i, :, lanes].astype(F32)
                win[1, i + 1, :, lanes] = mid
                win[0, i + 1, :, lanes] = jnp.where(
                    spot == 0, west_ref[0, i, :, lanes], pltpu.roll(mid, 1, 0)
                )
                win[2, i + 1, :, lanes] = jnp.where(
                    spot == side - 1, east_ref[0, i, :, lanes], pltpu.roll(mid, side - 1, 0)
                )
                return carry

            lax.fori_loop(0, side, shift, 0, unroll=2)

    @pl.when((step == 0) & (sample == 0))
    def _():
        sums_ref[...] = jnp.zeros_like(sums_ref)
        parts[...] = jnp.zeros_like(parts)

    cot = cot_ref[0].reshape(rows * side, channels)
    grad_act[...] = lax.dot_general(
        cot, point_ref[...], (((1,), (1,)), ((), ())), preferred_element_type=F32
    ).reshape(rows, side, channels)
    for lane in range(0, channels, HALF):
        lanes = pl.ds(lane, HALF)

        def row(k, held):
            held = list(held)
            i = step * rows + k
            for low in range(0, side, STRIP):
                spots = pl.ds(low, STRIP)
                views = [
                    win[col_off, i + row_off, spots, lanes]
                    for row_off in range(3)
                    for col_off in range(3)
                ]
                hidden = bias_ref[0:1, lanes] + taps_ref[0:1, lanes] * views[0]
                for t in range(1, 9):
                    hidden = hidden + taps_ref[t : t + 1, lanes] * views[t]
                output, slope = gelu_pair(hidden)
                act[k, spots, lanes] = output.astype(BF16)
                grad = (grad_act[k, spots, lanes] * slope).astype(BF16)
                g_ref[0, k, spots, lanes] = grad
                grad = grad.astype(F32)
                if low == 0:
                    gwest_ref[0, i, :, lanes] = grad[:1]
                if low + STRIP == side:
                    geast_ref[0, i, :, lanes] = grad[STRIP - 1 :]
                for t in range(9):
                    term = grad * views[t]
                    held[t] = held[t] + (term[:8] + term[8:])
                held[9] = held[9] + (grad[:8] + grad[8:])
            return tuple(held)

        held = lax.fori_loop(0, rows, row, tuple(parts[t, :, lanes] for t in range(10)))
        for t in range(10):
            parts[t, :, lanes] = held[t]
    sums_ref[0:channels] += lax.dot_general(
        act[...].reshape(rows * side, channels),
        cot,
        (((0,), (0,)), ((), ())),
        preferred_element_type=F32,
    )

    @pl.when((step == pl.num_programs(1) - 1) & (sample == pl.num_programs(0) - 1))
    def _():
        for t in range(10):
            sums_ref[channels + t : channels + t + 1] = jnp.sum(parts[t], axis=0, keepdims=True)
        sums_ref[...] = sums_ref[...] * norm_scale


def second_kernel(g_ref, north_ref, south_ref, west_ref, east_ref, taps_ref, out_ref):
    side, channels = g_ref.shape[1], g_ref.shape[3]
    spot = lax.broadcasted_iota(jnp.int32, (side, HALF), 0)
    for lane in range(0, channels, HALF):
        lanes = pl.ds(lane, HALF)

        def mixed(i, before, here, after):
            cols = [
                taps_ref[c : c + 1, lanes] * after
                + taps_ref[3 + c : 4 + c, lanes] * here
                + taps_ref[6 + c : 7 + c, lanes] * before
                for c in range(3)
            ]
            from_right = jnp.where(
                spot == side - 1, east_ref[0, i, :, lanes], pltpu.roll(cols[0], side - 1, 0)
            )
            from_left = jnp.where(
                spot == 0, west_ref[0, i, :, lanes], pltpu.roll(cols[2], 1, 0)
            )
            return cols[1] + from_right + from_left

        def load(i):
            return g_ref[0, i, :, lanes].astype(F32)

        empty = jnp.zeros((side, HALF), F32)
        first, second = load(0), load(1)
        out_ref[0, 0, :, lanes] = (
            mixed(0, empty, first, second) + north_ref[0, :, lanes].astype(F32)
        ).astype(BF16)

        def row(i, held):
            after = load(i + 1)
            out_ref[0, i, :, lanes] = mixed(i, held[0], held[1], after).astype(BF16)
            return held[1], after

        before, here = lax.fori_loop(1, side - 1, row, (first, second))
        out_ref[0, side - 1, :, lanes] = (
            mixed(side - 1, before, here, empty) + south_ref[0, :, lanes].astype(F32)
        ).astype(BF16)


def exchange(by_dir):
    face_count, tile_count = lax.axis_size("face"), lax.axis_size("tile")
    up = [(i, (i + 1) % face_count) for i in range(face_count)]
    right = [(i, (i + 1) % tile_count) for i in range(tile_count)]
    down = [(b, a) for a, b in up]
    left = [(b, a) for a, b in right]
    return jnp.stack(
        [
            lax.ppermute(by_dir[2], "face", up),
            lax.ppermute(by_dir[3], "tile", left),
            lax.ppermute(by_dir[0], "face", down),
            lax.ppermute(by_dir[1], "tile", right),
        ]
    )


def window_rows(first, row, last):
    row = jnp.concatenate([first[:, None], row, last[:, None]], axis=1)
    side = row.shape[1] - 2
    return jnp.stack([row[:, c : c + side] for c in range(3)], axis=1)


def end_windows(rim_rows, cmask):
    rim32 = rim_rows.astype(F32)
    north_west = (cmask[0] * 0.5 * (rim32[0][:, 0] + rim32[3][:, 0])).astype(BF16)
    north_east = (cmask[1] * 0.5 * (rim32[0][:, -1] + rim32[1][:, 0])).astype(BF16)
    south_east = (cmask[2] * 0.5 * (rim32[1][:, -1] + rim32[2][:, -1])).astype(BF16)
    south_west = (cmask[3] * 0.5 * (rim32[2][:, 0] + rim32[3][:, -1])).astype(BF16)
    return jnp.stack(
        [
            window_rows(north_west, rim_rows[0], north_east),
            window_rows(south_west, rim_rows[2], south_east),
        ],
        axis=1,
    )


def rim_terms(tap_rows, edges, mask_low, mask_high):
    length = edges.shape[2]
    spot = lax.broadcasted_iota(jnp.int32, (1, 1, length, 1), 2)
    padded_rows = jnp.pad(edges, ((0, 0), (0, 0), (1, 1), (0, 0)))
    tap_first = tap_rows[:, 0][:, None, None, :]
    tap_middle = tap_rows[:, 1][:, None, None, :]
    tap_last = tap_rows[:, 2][:, None, None, :]
    return (
        (tap_first * padded_rows[:, :, 2:] + tap_middle * edges)
        + tap_last * padded_rows[:, :, :-2]
        + jnp.where(spot == 0, (0.5 * mask_low) * tap_first * edges, 0.0)
        + jnp.where(spot == length - 1, (0.5 * mask_high) * tap_last * edges, 0.0)
    )


def shards(
    state_field,
    cotangent,
    depth_weight,
    depth_bias,
    point_weight,
    tile_links,
    link_sides,
    link_flips,
    corner_masks,
):
    batch, side, _, channels = state_field.shape
    face_count = lax.axis_size("face")
    tile_count = lax.axis_size("tile")
    face_pos = lax.axis_index("face")
    tile_pos = lax.axis_index("tile")
    toward = jnp.stack(
        [
            (face_pos - 1) % face_count * tile_count + tile_pos,
            face_pos * tile_count + (tile_pos + 1) % tile_count,
            (face_pos + 1) % face_count * tile_count + tile_pos,
            face_pos * tile_count + (tile_pos - 1) % tile_count,
        ]
    )
    matched = tile_links[0][:, None] == toward[None, :]
    counter = jnp.arange(4, dtype=jnp.int32)
    dir_of_side = jnp.sum(jnp.where(matched, counter[None, :], 0), axis=1)
    side_of_dir = jnp.sum(jnp.where(matched, counter[:, None], 0), axis=0)
    flip_side = (link_flips[0] == 1)[:, None, None, None]
    cmask = corner_masks[0].astype(F32)
    norm_scale = float(batch * side * side * face_count * tile_count) ** (-0.5)

    def swap(per_side):
        got = jnp.take(exchange(jnp.take(per_side, side_of_dir, axis=0)), dir_of_side, axis=0)
        return jnp.where(flip_side, got[:, :, ::-1], got)

    edges = jnp.stack(
        [state_field[:, 0], state_field[:, :, -1], state_field[:, -1], state_field[:, :, 0]]
    )
    rim_rows = swap(edges)
    ends = end_windows(rim_rows, cmask)

    whole = pl.BlockSpec((1, side, side, channels), lambda b, s: (b, 0, 0, 0))
    rows_of = pl.BlockSpec((1, ROWS, side, channels), lambda b, s: (b, s, 0, 0))
    line = pl.BlockSpec((1, side, 1, channels), lambda b, s: (b, 0, 0, 0))
    fixed = lambda *shape: pl.BlockSpec(shape, lambda b, s: (0,) * len(shape))
    pixels = batch * side * side
    sum_rows = channels + 16
    grad_hidden, grad_west, grad_east, sums = pl.pallas_call(
        functools.partial(first_kernel, norm_scale),
        grid=(batch, side // ROWS),
        in_specs=[
            whole,
            rows_of,
            pl.BlockSpec((1, 2, 3, side, channels), lambda b, s: (b, 0, 0, 0, 0)),
            line,
            line,
            fixed(9, channels),
            fixed(1, channels),
            fixed(channels, channels),
        ],
        out_specs=[rows_of, line, line, fixed(sum_rows, channels)],
        out_shape=[
            jax.ShapeDtypeStruct(state_field.shape, BF16),
            jax.ShapeDtypeStruct((batch, side, 1, channels), F32),
            jax.ShapeDtypeStruct((batch, side, 1, channels), F32),
            jax.ShapeDtypeStruct((sum_rows, channels), F32),
        ],
        scratch_shapes=[
            pltpu.VMEM((3, side + 2, side, channels), F32),
            pltpu.VMEM((ROWS, side, channels), F32),
            pltpu.VMEM((ROWS, side, channels), BF16),
            pltpu.VMEM((10, 8, channels), F32),
        ],
        compiler_params=pltpu.CompilerParams(vmem_limit_bytes=48 * 2**20),
        cost_estimate=pl.CostEstimate(
            flops=4 * pixels * channels * channels,
            bytes_accessed=6 * pixels * channels,
            transcendentals=pixels * channels,
        ),
    )(
        state_field,
        cotangent,
        ends,
        rim_rows[3].astype(F32)[:, :, None],
        rim_rows[1].astype(F32)[:, :, None],
        depth_weight,
        depth_bias[None],
        point_weight,
    )
    sums = lax.psum(sums, ("face", "tile"))

    tap_table = depth_weight.reshape(3, 3, channels)
    side_taps = jnp.stack([tap_table[0], tap_table[:, 2], tap_table[2], tap_table[:, 0]], axis=0)
    mask_low = cmask[jnp.array([0, 1, 3, 0])][:, None, None, None]
    mask_high = cmask[jnp.array([1, 2, 2, 3])][:, None, None, None]
    grad_edges = jnp.stack(
        [
            grad_hidden[:, 0].astype(F32),
            grad_east[:, :, 0],
            grad_hidden[:, -1].astype(F32),
            grad_west[:, :, 0],
        ]
    )
    incoming = swap(rim_terms(side_taps, grad_edges, mask_low, mask_high).astype(BF16))

    whole = pl.BlockSpec((1, side, side, channels), lambda b: (b, 0, 0, 0))
    line = pl.BlockSpec((1, side, 1, channels), lambda b: (b, 0, 0, 0))
    flat = pl.BlockSpec((1, side, channels), lambda b: (b, 0, 0))
    field_grad = pl.pallas_call(
        second_kernel,
        grid=(batch,),
        in_specs=[whole, flat, flat, line, line, pl.BlockSpec((9, channels), lambda b: (0, 0))],
        out_specs=whole,
        out_shape=jax.ShapeDtypeStruct(state_field.shape, BF16),
        compiler_params=pltpu.CompilerParams(vmem_limit_bytes=48 * 2**20),
        cost_estimate=pl.CostEstimate(
            flops=40 * pixels * channels,
            bytes_accessed=4 * pixels * channels,
            transcendentals=0,
        ),
    )(
        grad_hidden,
        incoming[0],
        incoming[2],
        incoming[3].astype(F32)[:, :, None],
        incoming[1].astype(F32)[:, :, None],
        depth_weight,
    )
    return (
        field_grad,
        sums[channels : channels + 9],
        sums[channels + 9],
        sums[:channels],
    )


def solution(mesh):
    in_specs = (
        P(None, "face", "tile", None),
        P(None, "face", "tile", None),
        P(),
        P(),
        P(),
        P(("face", "tile"), None),
        P(("face", "tile"), None),
        P(("face", "tile"), None),
        P(("face", "tile"), None),
    )
    out_specs = (P(None, "face", "tile", None), P(), P(), P())
    return jax.shard_map(shards, mesh=mesh, in_specs=in_specs, out_specs=out_specs, check_vma=False)
```

```python
import functools

import jax
import jax.numpy as jnp
from jax import lax
from jax.experimental import pallas as pl
from jax.experimental.pallas import tpu as pltpu
from jax.sharding import PartitionSpec as P

root_two_pi = 0.7978845608028654
cubic_coef = 0.044715
HALF = 128
STRIP = 16
ROWS = 16
F32 = jnp.float32
BF16 = jnp.bfloat16


def gelu_pair(hidden):
    square = hidden * hidden
    gate = 0.5 + 0.5 * jnp.tanh(hidden * (root_two_pi + (root_two_pi * cubic_coef) * square))
    output = hidden * gate
    slope = gate + output * (1.0 - gate) * (
        2.0 * root_two_pi + (6.0 * root_two_pi * cubic_coef) * square
    )
    return output, slope


def first_kernel(
    norm_scale,
    x_ref,
    cot_ref,
    ends_ref,
    west_ref,
    east_ref,
    taps_ref,
    bias_ref,
    point_ref,
    g_ref,
    gnorth_ref,
    gsouth_ref,
    gwest_ref,
    geast_ref,
    sums_ref,
    win,
    grad_act,
    act,
    parts,
):
    sample, step = pl.program_id(0), pl.program_id(1)
    side, channels = x_ref.shape[1], x_ref.shape[3]
    rows = cot_ref.shape[1]

    @pl.when(step == 0)
    def _():
        for col_off in range(3):
            win[col_off, 0] = ends_ref[0, 0, col_off].astype(F32)
            win[col_off, side + 1] = ends_ref[0, 1, col_off].astype(F32)
        spot = lax.broadcasted_iota(jnp.int32, (side, HALF), 0)
        for lane in range(0, channels, HALF):
            lanes = pl.ds(lane, HALF)

            def shift(i, carry):
                mid = x_ref[0, i, :, lanes].astype(F32)
                win[1, i + 1, :, lanes] = mid
                win[0, i + 1, :, lanes] = jnp.where(
                    spot == 0, west_ref[0, i, :, lanes], pltpu.roll(mid, 1, 0)
                )
                win[2, i + 1, :, lanes] = jnp.where(
                    spot == side - 1, east_ref[0, i, :, lanes], pltpu.roll(mid, side - 1, 0)
                )
                return carry

            lax.fori_loop(0, side, shift, 0, unroll=2)

    @pl.when((step == 0) & (sample == 0))
    def _():
        sums_ref[...] = jnp.zeros_like(sums_ref)
        parts[...] = jnp.zeros_like(parts)

    cot = cot_ref[0].reshape(rows * side, channels)
    grad_act[...] = lax.dot_general(
        cot, point_ref[...], (((1,), (1,)), ((), ())), preferred_element_type=F32
    ).reshape(rows, side, channels)
    for lane in range(0, channels, HALF):
        lanes = pl.ds(lane, HALF)

        def row(k, held):
            held = list(held)
            i = step * rows + k
            for low in range(0, side, STRIP):
                spots = pl.ds(low, STRIP)
                views = [
                    win[col_off, i + row_off, spots, lanes]
                    for row_off in range(3)
                    for col_off in range(3)
                ]
                hidden = bias_ref[0:1, lanes] + taps_ref[0:1, lanes] * views[0]
                for t in range(1, 9):
                    hidden = hidden + taps_ref[t : t + 1, lanes] * views[t]
                output, slope = gelu_pair(hidden)
                act[k, spots, lanes] = output.astype(BF16)
                grad = (grad_act[k, spots, lanes] * slope).astype(BF16)
                g_ref[0, k, spots, lanes] = grad
                grad = grad.astype(F32)
                if low == 0:
                    gwest_ref[0, i, :, lanes] = grad[:1]
                if low + STRIP == side:
                    geast_ref[0, i, :, lanes] = grad[STRIP - 1 :]
                for t in range(9):
                    term = grad * views[t]
                    held[t] = held[t] + (term[:8] + term[8:])
                held[9] = held[9] + (grad[:8] + grad[8:])
            return tuple(held)

        held = lax.fori_loop(0, rows, row, tuple(parts[t, :, lanes] for t in range(10)))
        for t in range(10):
            parts[t, :, lanes] = held[t]
    sums_ref[0:channels] += lax.dot_general(
        act[...].reshape(rows * side, channels),
        cot,
        (((0,), (0,)), ((), ())),
        preferred_element_type=F32,
    )

    @pl.when(step == 0)
    def _():
        gnorth_ref[0] = g_ref[0, 0].astype(F32)

    @pl.when(step == pl.num_programs(1) - 1)
    def _():
        gsouth_ref[0] = g_ref[0, rows - 1].astype(F32)

    @pl.when((step == pl.num_programs(1) - 1) & (sample == pl.num_programs(0) - 1))
    def _():
        for t in range(10):
            sums_ref[channels + t : channels + t + 1] = jnp.sum(parts[t], axis=0, keepdims=True)
        sums_ref[...] = sums_ref[...] * norm_scale


def second_kernel(g_ref, north_ref, south_ref, west_ref, east_ref, taps_ref, out_ref):
    side, channels = g_ref.shape[1], g_ref.shape[3]
    spot = lax.broadcasted_iota(jnp.int32, (side, HALF), 0)
    for lane in range(0, channels, HALF):
        lanes = pl.ds(lane, HALF)

        def mixed(i, before, here, after):
            cols = [
                taps_ref[c : c + 1, lanes] * after
                + taps_ref[3 + c : 4 + c, lanes] * here
                + taps_ref[6 + c : 7 + c, lanes] * before
                for c in range(3)
            ]
            from_right = jnp.where(
                spot == side - 1, east_ref[0, i, :, lanes], pltpu.roll(cols[0], side - 1, 0)
            )
            from_left = jnp.where(
                spot == 0, west_ref[0, i, :, lanes], pltpu.roll(cols[2], 1, 0)
            )
            return cols[1] + from_right + from_left

        def load(i):
            return g_ref[0, i, :, lanes].astype(F32)

        empty = jnp.zeros((side, HALF), F32)
        first, second = load(0), load(1)
        out_ref[0, 0, :, lanes] = (
            mixed(0, empty, first, second) + north_ref[0, :, lanes].astype(F32)
        ).astype(BF16)

        def row(i, held):
            after = load(i + 1)
            out_ref[0, i, :, lanes] = mixed(i, held[0], held[1], after).astype(BF16)
            return held[1], after

        before, here = lax.fori_loop(1, side - 1, row, (first, second))
        out_ref[0, side - 1, :, lanes] = (
            mixed(side - 1, before, here, empty) + south_ref[0, :, lanes].astype(F32)
        ).astype(BF16)


def exchange(by_dir):
    face_count, tile_count = lax.axis_size("face"), lax.axis_size("tile")
    up = [(i, (i + 1) % face_count) for i in range(face_count)]
    right = [(i, (i + 1) % tile_count) for i in range(tile_count)]
    down = [(b, a) for a, b in up]
    left = [(b, a) for a, b in right]
    return jnp.stack(
        [
            lax.ppermute(by_dir[2], "face", up),
            lax.ppermute(by_dir[3], "tile", left),
            lax.ppermute(by_dir[0], "face", down),
            lax.ppermute(by_dir[1], "tile", right),
        ]
    )


def comm_kernel(
    face_count,
    tile_count,
    leaving_ref,
    sums_ref,
    returned_ref,
    point_ref,
    depth_ref,
    bias_ref,
    rims,
    face_box,
    face_extra,
    tile_box,
    tile_extra,
    part,
    extra,
    total,
    rim_send,
    rim_recv,
    face_send,
    face_recv,
    face_xsend,
    face_xrecv,
    tile_send,
    tile_recv,
    tile_xsend,
    tile_xrecv,
    tile_gsend,
    tile_grecv,
    face_gsend,
    face_grecv,
):
    face, tile = lax.axis_index("face"), lax.axis_index("tile")
    channels = point_ref.shape[0]
    block = channels // face_count
    owners = min(tile_count, block // 8)
    piece = block // owners

    def copy(src, dst, send_sem, recv_sem, to_face, to_tile):
        return pltpu.make_async_remote_copy(
            src_ref=src,
            dst_ref=dst,
            send_sem=send_sem,
            recv_sem=recv_sem,
            device_id=(to_face, to_tile),
            device_id_type=pl.DeviceIdType.MESH,
        )

    faces = [
        (k, lax.rem(face + k, face_count), lax.rem(face + face_count - k, face_count))
        for k in range(1, face_count)
    ]
    tiles = [
        (k, lax.rem(tile + k, tile_count), lax.rem(tile + tile_count - k, tile_count))
        for k in range(1, tile_count)
    ]

    barrier = pltpu.get_barrier_semaphore()
    for _, to, _ in faces:
        pl.semaphore_signal(
            barrier, inc=1, device_id=(to, tile), device_id_type=pl.DeviceIdType.MESH
        )
    for _, to, _ in tiles:
        pl.semaphore_signal(
            barrier, inc=1, device_id=(face, to), device_id_type=pl.DeviceIdType.MESH
        )
    pl.semaphore_wait(barrier, face_count + tile_count - 2)

    def rows_of(index, size):
        return pl.ds(pl.multiple_of(index * size, 8), size)

    sent = []
    for k, to, _ in faces:
        sent.append(
            copy(
                sums_ref.at[rows_of(to, block)],
                face_box.at[face],
                face_send.at[k],
                face_recv.at[face],
                to,
                tile,
            )
        )
        sent.append(
            copy(
                sums_ref.at[pl.ds(channels, 16)],
                face_extra.at[face],
                face_xsend.at[k],
                face_xrecv.at[face],
                to,
                tile,
            )
        )
    up, down = lax.rem(face + face_count - 1, face_count), lax.rem(face + 1, face_count)
    left, right = lax.rem(tile + tile_count - 1, tile_count), lax.rem(tile + 1, tile_count)
    rim_copies = [
        copy(leaving_ref.at[d], rims.at[(d + 2) % 4], rim_send.at[d], rim_recv.at[(d + 2) % 4], *to)
        for d, to in enumerate([(up, tile), (face, right), (down, tile), (face, left)])
    ]
    for one in sent + rim_copies:
        one.start()
    face_box[face] = sums_ref[rows_of(face, block)]
    face_extra[face] = sums_ref[channels : channels + 16]
    for k, to, source in faces:
        copy(
            face_box.at[source], face_box.at[source], face_send.at[k], face_recv.at[source], to, tile
        ).wait_recv()
        copy(
            face_extra.at[source],
            face_extra.at[source],
            face_xsend.at[k],
            face_xrecv.at[source],
            to,
            tile,
        ).wait_recv()
    acc, small = face_box[0], face_extra[0]
    for f in range(1, face_count):
        acc, small = acc + face_box[f], small + face_extra[f]
    part[...] = acc
    extra[...] = small

    for k, to, _ in tiles:

        @pl.when(to < owners)
        def _():
            copy(
                part.at[rows_of(to, piece)],
                tile_box.at[tile],
                tile_send.at[k],
                tile_recv.at[tile],
                face,
                to,
            ).start()

        one = copy(
            extra, tile_extra.at[tile], tile_xsend.at[k], tile_xrecv.at[tile], face, to
        )
        one.start()
        sent.append(one)
    tile_extra[tile] = extra[...]

    @pl.when(tile < owners)
    def _():
        tile_box[tile] = part[rows_of(tile, piece)]
        for k, to, source in tiles:
            copy(
                tile_box.at[source],
                tile_box.at[source],
                tile_send.at[k],
                tile_recv.at[source],
                face,
                to,
            ).wait_recv()
        acc = tile_box[0]
        for t in range(1, tile_count):
            acc = acc + tile_box[t]
        mine = rows_of(face * owners + tile, piece)
        total[mine] = acc
        for k, to, _ in tiles:
            copy(
                total.at[mine], total.at[mine], tile_gsend.at[k], tile_grecv.at[tile], face, to
            ).start()

    for k, to, source in tiles:

        @pl.when(source < owners)
        def _():
            theirs = rows_of(face * owners + source, piece)
            copy(
                total.at[theirs], total.at[theirs], tile_gsend.at[k], tile_grecv.at[source], face, to
            ).wait_recv()

    mine = rows_of(face, block)
    for k, to, _ in faces:
        one = copy(total.at[mine], total.at[mine], face_gsend.at[k], face_grecv.at[face], to, tile)
        one.start()
        sent.append(one)
    for k, to, source in tiles:
        copy(
            tile_extra.at[source],
            tile_extra.at[source],
            tile_xsend.at[k],
            tile_xrecv.at[source],
            face,
            to,
        ).wait_recv()
    small = tile_extra[0]
    for t in range(1, tile_count):
        small = small + tile_extra[t]
    depth_ref[...] = small[:9]
    bias_ref[...] = small[9:10]
    for one in rim_copies:
        one.wait_recv()
    returned_ref[...] = rims[...]
    for k, to, source in faces:
        theirs = rows_of(source, block)
        copy(
            total.at[theirs], total.at[theirs], face_gsend.at[k], face_grecv.at[source], to, tile
        ).wait_recv()
    point_ref[...] = total[...]
    for one in sent + rim_copies:
        one.wait_send()
    for k, to, _ in tiles:

        @pl.when(to < owners)
        def _():
            copy(
                part.at[rows_of(to, piece)],
                tile_box.at[tile],
                tile_send.at[k],
                tile_recv.at[tile],
                face,
                to,
            ).wait_send()

        @pl.when(tile < owners)
        def _():
            own = rows_of(face * owners + tile, piece)
            copy(
                total.at[own], total.at[own], tile_gsend.at[k], tile_grecv.at[tile], face, to
            ).wait_send()


def return_and_sum(leaving, sums):
    face_count, tile_count = lax.axis_size("face"), lax.axis_size("tile")
    channels = sums.shape[1]
    block = channels // face_count
    piece = block // min(tile_count, block // 8)
    vmem = pl.BlockSpec(memory_space=pltpu.VMEM)
    dma = pltpu.SemaphoreType.DMA
    return pl.pallas_call(
        functools.partial(comm_kernel, face_count, tile_count),
        in_specs=[vmem, vmem],
        out_specs=[vmem] * 4,
        out_shape=[
            jax.ShapeDtypeStruct(leaving.shape, BF16),
            jax.ShapeDtypeStruct((channels, channels), F32),
            jax.ShapeDtypeStruct((9, channels), F32),
            jax.ShapeDtypeStruct((1, channels), F32),
        ],
        scratch_shapes=[
            pltpu.VMEM(leaving.shape, BF16),
            pltpu.VMEM((face_count, block, channels), F32),
            pltpu.VMEM((face_count, 16, channels), F32),
            pltpu.VMEM((tile_count, piece, channels), F32),
            pltpu.VMEM((tile_count, 16, channels), F32),
            pltpu.VMEM((block, channels), F32),
            pltpu.VMEM((16, channels), F32),
            pltpu.VMEM((channels, channels), F32),
            dma((4,)),
            dma((4,)),
        ]
        + [dma((face_count,))] * 4
        + [dma((tile_count,))] * 6
        + [dma((face_count,))] * 2,
        compiler_params=pltpu.CompilerParams(
            collective_id=0, has_side_effects=True, vmem_limit_bytes=32 * 2**20
        ),
    )(leaving, sums)


def window_rows(first, row, last):
    row = jnp.concatenate([first[:, None], row, last[:, None]], axis=1)
    side = row.shape[1] - 2
    return jnp.stack([row[:, c : c + side] for c in range(3)], axis=1)


def end_windows(rim_rows, cmask):
    rim32 = rim_rows.astype(F32)
    north_west = (cmask[0] * 0.5 * (rim32[0][:, 0] + rim32[3][:, 0])).astype(BF16)
    north_east = (cmask[1] * 0.5 * (rim32[0][:, -1] + rim32[1][:, 0])).astype(BF16)
    south_east = (cmask[2] * 0.5 * (rim32[1][:, -1] + rim32[2][:, -1])).astype(BF16)
    south_west = (cmask[3] * 0.5 * (rim32[2][:, 0] + rim32[3][:, -1])).astype(BF16)
    return jnp.stack(
        [
            window_rows(north_west, rim_rows[0], north_east),
            window_rows(south_west, rim_rows[2], south_east),
        ],
        axis=1,
    )


def rim_terms(tap_rows, edges, mask_low, mask_high):
    length = edges.shape[2]
    spot = lax.broadcasted_iota(jnp.int32, (1, 1, length, 1), 2)
    padded_rows = jnp.pad(edges, ((0, 0), (0, 0), (1, 1), (0, 0)))
    tap_first = tap_rows[:, 0][:, None, None, :]
    tap_middle = tap_rows[:, 1][:, None, None, :]
    tap_last = tap_rows[:, 2][:, None, None, :]
    return (
        (tap_first * padded_rows[:, :, 2:] + tap_middle * edges)
        + tap_last * padded_rows[:, :, :-2]
        + jnp.where(spot == 0, (0.5 * mask_low) * tap_first * edges, 0.0)
        + jnp.where(spot == length - 1, (0.5 * mask_high) * tap_last * edges, 0.0)
    )


def shards(
    state_field,
    cotangent,
    depth_weight,
    depth_bias,
    point_weight,
    tile_links,
    link_sides,
    link_flips,
    corner_masks,
):
    batch, side, _, channels = state_field.shape
    face_count = lax.axis_size("face")
    tile_count = lax.axis_size("tile")
    face_pos = lax.axis_index("face")
    tile_pos = lax.axis_index("tile")
    toward = jnp.stack(
        [
            (face_pos - 1) % face_count * tile_count + tile_pos,
            face_pos * tile_count + (tile_pos + 1) % tile_count,
            (face_pos + 1) % face_count * tile_count + tile_pos,
            face_pos * tile_count + (tile_pos - 1) % tile_count,
        ]
    )
    matched = tile_links[0][:, None] == toward[None, :]
    counter = jnp.arange(4, dtype=jnp.int32)
    dir_of_side = jnp.sum(jnp.where(matched, counter[None, :], 0), axis=1)
    side_of_dir = jnp.sum(jnp.where(matched, counter[:, None], 0), axis=0)
    flip_side = (link_flips[0] == 1)[:, None, None, None]
    cmask = corner_masks[0].astype(F32)
    norm_scale = float(batch * side * side * face_count * tile_count) ** (-0.5)

    def toward_sides(by_dir):
        got = jnp.take(by_dir, dir_of_side, axis=0)
        return jnp.where(flip_side, got[:, :, ::-1], got)

    edges = jnp.stack(
        [state_field[:, 0], state_field[:, :, -1], state_field[:, -1], state_field[:, :, 0]]
    )
    rim_rows = toward_sides(exchange(jnp.take(edges, side_of_dir, axis=0)))
    ends = end_windows(rim_rows, cmask)

    whole = pl.BlockSpec((1, side, side, channels), lambda b, s: (b, 0, 0, 0))
    rows_of = pl.BlockSpec((1, ROWS, side, channels), lambda b, s: (b, s, 0, 0))
    line = pl.BlockSpec((1, side, 1, channels), lambda b, s: (b, 0, 0, 0))
    flat = pl.BlockSpec((1, side, channels), lambda b, s: (b, 0, 0))
    fixed = lambda *shape: pl.BlockSpec(shape, lambda b, s: (0,) * len(shape))
    pixels = batch * side * side
    sum_rows = channels + 16
    grad_hidden, grad_north, grad_south, grad_west, grad_east, sums = pl.pallas_call(
        functools.partial(first_kernel, norm_scale),
        grid=(batch, side // ROWS),
        in_specs=[
            whole,
            rows_of,
            pl.BlockSpec((1, 2, 3, side, channels), lambda b, s: (b, 0, 0, 0, 0)),
            line,
            line,
            fixed(9, channels),
            fixed(1, channels),
            fixed(channels, channels),
        ],
        out_specs=[rows_of, flat, flat, line, line, fixed(sum_rows, channels)],
        out_shape=[
            jax.ShapeDtypeStruct(state_field.shape, BF16),
            jax.ShapeDtypeStruct((batch, side, channels), F32),
            jax.ShapeDtypeStruct((batch, side, channels), F32),
            jax.ShapeDtypeStruct((batch, side, 1, channels), F32),
            jax.ShapeDtypeStruct((batch, side, 1, channels), F32),
            jax.ShapeDtypeStruct((sum_rows, channels), F32),
        ],
        scratch_shapes=[
            pltpu.VMEM((3, side + 2, side, channels), F32),
            pltpu.VMEM((ROWS, side, channels), F32),
            pltpu.VMEM((ROWS, side, channels), BF16),
            pltpu.VMEM((10, 8, channels), F32),
        ],
        compiler_params=pltpu.CompilerParams(vmem_limit_bytes=48 * 2**20),
        cost_estimate=pl.CostEstimate(
            flops=4 * pixels * channels * channels,
            bytes_accessed=6 * pixels * channels,
            transcendentals=pixels * channels,
        ),
    )(
        state_field,
        cotangent,
        ends,
        rim_rows[3].astype(F32)[:, :, None],
        rim_rows[1].astype(F32)[:, :, None],
        depth_weight,
        depth_bias[None],
        point_weight,
    )

    tap_table = depth_weight.reshape(3, 3, channels)
    side_taps = jnp.stack([tap_table[0], tap_table[:, 2], tap_table[2], tap_table[:, 0]], axis=0)
    mask_low = cmask[jnp.array([0, 1, 3, 0])][:, None, None, None]
    mask_high = cmask[jnp.array([1, 2, 2, 3])][:, None, None, None]
    grad_edges = jnp.stack(
        [
            grad_north,
            grad_east[:, :, 0],
            grad_south,
            grad_west[:, :, 0],
        ]
    )
    leaving = rim_terms(side_taps, grad_edges, mask_low, mask_high).astype(BF16)
    leaving = jnp.take(leaving, side_of_dir, axis=0)
    returned, point_sum, depth_sum, bias_sum = return_and_sum(
        leaving.reshape(4, batch * side, channels), sums
    )
    incoming = toward_sides(returned.reshape(leaving.shape))

    whole = pl.BlockSpec((1, side, side, channels), lambda b: (b, 0, 0, 0))
    line = pl.BlockSpec((1, side, 1, channels), lambda b: (b, 0, 0, 0))
    flat = pl.BlockSpec((1, side, channels), lambda b: (b, 0, 0))
    field_grad = pl.pallas_call(
        second_kernel,
        grid=(batch,),
        in_specs=[whole, flat, flat, line, line, pl.BlockSpec((9, channels), lambda b: (0, 0))],
        out_specs=whole,
        out_shape=jax.ShapeDtypeStruct(state_field.shape, BF16),
        compiler_params=pltpu.CompilerParams(vmem_limit_bytes=48 * 2**20),
        cost_estimate=pl.CostEstimate(
            flops=40 * pixels * channels,
            bytes_accessed=4 * pixels * channels,
            transcendentals=0,
        ),
    )(
        grad_hidden,
        incoming[0],
        incoming[2],
        incoming[3].astype(F32)[:, :, None],
        incoming[1].astype(F32)[:, :, None],
        depth_weight,
    )
    return field_grad, depth_sum, bias_sum[0], point_sum


def solution(mesh):
    in_specs = (
        P(None, "face", "tile", None),
        P(None, "face", "tile", None),
        P(),
        P(),
        P(),
        P(("face", "tile"), None),
        P(("face", "tile"), None),
        P(("face", "tile"), None),
        P(("face", "tile"), None),
    )
    out_specs = (P(None, "face", "tile", None), P(), P(), P())
    return jax.shard_map(shards, mesh=mesh, in_specs=in_specs, out_specs=out_specs, check_vma=False)
```

```python
import functools

import jax
import jax.numpy as jnp
from jax import lax
from jax.experimental import pallas as pl
from jax.experimental.pallas import tpu as pltpu
from jax.sharding import PartitionSpec as P

root_two_pi = 0.7978845608028654
cubic_coef = 0.044715
HALF = 128
STRIP = 16
ROWS = 16
F32 = jnp.float32
BF16 = jnp.bfloat16


def gelu_pair(hidden):
    square = hidden * hidden
    gate = 0.5 + 0.5 * jnp.tanh(hidden * (root_two_pi + (root_two_pi * cubic_coef) * square))
    output = hidden * gate
    slope = gate + output * (1.0 - gate) * (
        2.0 * root_two_pi + (6.0 * root_two_pi * cubic_coef) * square
    )
    return output, slope


def rim_of_side(by_dir_ref, links_ref, s):
    rows = by_dir_ref[links_ref[0, s], 0]
    side = rows.shape[0]
    spots = [lax.broadcasted_iota(jnp.int32, (side, side), axis) for axis in range(2)]
    swap = jnp.where(spots[0] + spots[1] == side - 1, 1.0, 0.0).astype(BF16)
    turned = jnp.dot(swap, rows, preferred_element_type=F32)
    return jnp.where(jnp.full(rows.shape, links_ref[1, s]) == 1, turned, rows.astype(F32))


def into_lines(lines_ref, rows):
    for i in range(rows.shape[0]):
        lines_ref[i] = rows[i : i + 1]


def first_kernel(
    norm_scale,
    x_ref,
    cot_ref,
    rims_ref,
    links_ref,
    taps_ref,
    bias_ref,
    point_ref,
    g_ref,
    gnorth_ref,
    gsouth_ref,
    gwest_ref,
    geast_ref,
    sums_ref,
    win,
    grad_act,
    act,
    parts,
    west,
    east,
):
    sample, step = pl.program_id(0), pl.program_id(1)
    side, channels = x_ref.shape[1], x_ref.shape[3]
    rows = cot_ref.shape[1]

    @pl.when(step == 0)
    def _():
        rims = [rim_of_side(rims_ref, links_ref, s) for s in range(4)]
        into_lines(west, rims[3])
        into_lines(east, rims[1])

        def corner(c, one, other):
            mask = jnp.full((1, channels), links_ref[2, c]).astype(F32)
            return (mask * 0.5 * (one + other)).astype(BF16).astype(F32)

        north_west = corner(0, rims[0][:1], rims[3][:1])
        north_east = corner(1, rims[0][side - 1 :], rims[1][:1])
        south_east = corner(2, rims[1][side - 1 :], rims[2][side - 1 :])
        south_west = corner(3, rims[2][:1], rims[3][side - 1 :])
        spot = lax.broadcasted_iota(jnp.int32, (side, channels), 0)
        for at, rim, low, high in (
            (0, rims[0], north_west, north_east),
            (side + 1, rims[2], south_west, south_east),
        ):
            win[0, at] = jnp.where(spot == 0, low, pltpu.roll(rim, 1, 0))
            win[1, at] = rim
            win[2, at] = jnp.where(spot == side - 1, high, pltpu.roll(rim, side - 1, 0))
        spot = lax.broadcasted_iota(jnp.int32, (side, HALF), 0)
        for lane in range(0, channels, HALF):
            lanes = pl.ds(lane, HALF)

            def shift(i, carry):
                mid = x_ref[0, i, :, lanes].astype(F32)
                win[1, i + 1, :, lanes] = mid
                win[0, i + 1, :, lanes] = jnp.where(
                    spot == 0, west[i, :, lanes], pltpu.roll(mid, 1, 0)
                )
                win[2, i + 1, :, lanes] = jnp.where(
                    spot == side - 1, east[i, :, lanes], pltpu.roll(mid, side - 1, 0)
                )
                return carry

            lax.fori_loop(0, side, shift, 0, unroll=2)

    @pl.when((step == 0) & (sample == 0))
    def _():
        sums_ref[...] = jnp.zeros_like(sums_ref)
        parts[...] = jnp.zeros_like(parts)

    cot = cot_ref[0].reshape(rows * side, channels)
    grad_act[...] = lax.dot_general(
        cot, point_ref[...], (((1,), (1,)), ((), ())), preferred_element_type=F32
    ).reshape(rows, side, channels)
    for lane in range(0, channels, HALF):
        lanes = pl.ds(lane, HALF)

        def row(k, held):
            held = list(held)
            i = step * rows + k
            for low in range(0, side, STRIP):
                spots = pl.ds(low, STRIP)
                views = [
                    win[col_off, i + row_off, spots, lanes]
                    for row_off in range(3)
                    for col_off in range(3)
                ]
                hidden = bias_ref[0:1, lanes] + taps_ref[0:1, lanes] * views[0]
                for t in range(1, 9):
                    hidden = hidden + taps_ref[t : t + 1, lanes] * views[t]
                output, slope = gelu_pair(hidden)
                act[k, spots, lanes] = output.astype(BF16)
                grad = (grad_act[k, spots, lanes] * slope).astype(BF16)
                g_ref[0, k, spots, lanes] = grad
                grad = grad.astype(F32)
                if low == 0:
                    gwest_ref[0, i, :, lanes] = grad[:1]
                if low + STRIP == side:
                    geast_ref[0, i, :, lanes] = grad[STRIP - 1 :]
                for t in range(9):
                    term = grad * views[t]
                    held[t] = held[t] + (term[:8] + term[8:])
                held[9] = held[9] + (grad[:8] + grad[8:])
            return tuple(held)

        held = lax.fori_loop(0, rows, row, tuple(parts[t, :, lanes] for t in range(10)))
        for t in range(10):
            parts[t, :, lanes] = held[t]
    sums_ref[0:channels] += lax.dot_general(
        act[...].reshape(rows * side, channels),
        cot,
        (((0,), (0,)), ((), ())),
        preferred_element_type=F32,
    )

    @pl.when(step == 0)
    def _():
        gnorth_ref[0] = g_ref[0, 0].astype(F32)

    @pl.when(step == pl.num_programs(1) - 1)
    def _():
        gsouth_ref[0] = g_ref[0, rows - 1].astype(F32)

    @pl.when((step == pl.num_programs(1) - 1) & (sample == pl.num_programs(0) - 1))
    def _():
        for t in range(10):
            sums_ref[channels + t : channels + t + 1] = jnp.sum(parts[t], axis=0, keepdims=True)
        sums_ref[...] = sums_ref[...] * norm_scale


def second_kernel(g_ref, rims_ref, links_ref, taps_ref, out_ref, north, south, west, east):
    side, channels = g_ref.shape[1], g_ref.shape[3]
    north[...] = rim_of_side(rims_ref, links_ref, 0)
    into_lines(east, rim_of_side(rims_ref, links_ref, 1))
    south[...] = rim_of_side(rims_ref, links_ref, 2)
    into_lines(west, rim_of_side(rims_ref, links_ref, 3))
    spot = lax.broadcasted_iota(jnp.int32, (side, HALF), 0)
    for lane in range(0, channels, HALF):
        lanes = pl.ds(lane, HALF)

        def mixed(i, before, here, after):
            cols = [
                taps_ref[c : c + 1, lanes] * after
                + taps_ref[3 + c : 4 + c, lanes] * here
                + taps_ref[6 + c : 7 + c, lanes] * before
                for c in range(3)
            ]
            from_right = jnp.where(
                spot == side - 1, east[i, :, lanes], pltpu.roll(cols[0], side - 1, 0)
            )
            from_left = jnp.where(
                spot == 0, west[i, :, lanes], pltpu.roll(cols[2], 1, 0)
            )
            return cols[1] + from_right + from_left

        def load(i):
            return g_ref[0, i, :, lanes].astype(F32)

        empty = jnp.zeros((side, HALF), F32)
        first, second = load(0), load(1)
        out_ref[0, 0, :, lanes] = (
            mixed(0, empty, first, second) + north[:, lanes]
        ).astype(BF16)

        def row(i, held):
            after = load(i + 1)
            out_ref[0, i, :, lanes] = mixed(i, held[0], held[1], after).astype(BF16)
            return held[1], after

        before, here = lax.fori_loop(1, side - 1, row, (first, second))
        out_ref[0, side - 1, :, lanes] = (
            mixed(side - 1, before, here, empty) + south[:, lanes]
        ).astype(BF16)


def exchange(by_dir):
    face_count, tile_count = lax.axis_size("face"), lax.axis_size("tile")
    up = [(i, (i + 1) % face_count) for i in range(face_count)]
    right = [(i, (i + 1) % tile_count) for i in range(tile_count)]
    down = [(b, a) for a, b in up]
    left = [(b, a) for a, b in right]
    return jnp.stack(
        [
            lax.ppermute(by_dir[2], "face", up),
            lax.ppermute(by_dir[3], "tile", left),
            lax.ppermute(by_dir[0], "face", down),
            lax.ppermute(by_dir[1], "tile", right),
        ]
    )


def comm_kernel(
    face_count,
    tile_count,
    leaving_ref,
    sums_ref,
    returned_ref,
    point_ref,
    depth_ref,
    bias_ref,
    rims,
    face_box,
    face_extra,
    tile_box,
    tile_extra,
    part,
    extra,
    total,
    rim_send,
    rim_recv,
    face_send,
    face_recv,
    face_xsend,
    face_xrecv,
    tile_send,
    tile_recv,
    tile_xsend,
    tile_xrecv,
    tile_gsend,
    tile_grecv,
    face_gsend,
    face_grecv,
):
    face, tile = lax.axis_index("face"), lax.axis_index("tile")
    channels = point_ref.shape[0]
    block = channels // face_count
    owners = min(tile_count, block // 8)
    piece = block // owners

    def copy(src, dst, send_sem, recv_sem, to_face, to_tile):
        return pltpu.make_async_remote_copy(
            src_ref=src,
            dst_ref=dst,
            send_sem=send_sem,
            recv_sem=recv_sem,
            device_id=(to_face, to_tile),
            device_id_type=pl.DeviceIdType.MESH,
        )

    faces = [
        (k, lax.rem(face + k, face_count), lax.rem(face + face_count - k, face_count))
        for k in range(1, face_count)
    ]
    tiles = [
        (k, lax.rem(tile + k, tile_count), lax.rem(tile + tile_count - k, tile_count))
        for k in range(1, tile_count)
    ]

    barrier = pltpu.get_barrier_semaphore()
    for _, to, _ in faces:
        pl.semaphore_signal(
            barrier, inc=1, device_id=(to, tile), device_id_type=pl.DeviceIdType.MESH
        )
    for _, to, _ in tiles:
        pl.semaphore_signal(
            barrier, inc=1, device_id=(face, to), device_id_type=pl.DeviceIdType.MESH
        )
    pl.semaphore_wait(barrier, face_count + tile_count - 2)

    def rows_of(index, size):
        return pl.ds(pl.multiple_of(index * size, 8), size)

    sent = []
    for k, to, _ in faces:
        sent.append(
            copy(
                sums_ref.at[rows_of(to, block)],
                face_box.at[face],
                face_send.at[k],
                face_recv.at[face],
                to,
                tile,
            )
        )
        sent.append(
            copy(
                sums_ref.at[pl.ds(channels, 16)],
                face_extra.at[face],
                face_xsend.at[k],
                face_xrecv.at[face],
                to,
                tile,
            )
        )
    up, down = lax.rem(face + face_count - 1, face_count), lax.rem(face + 1, face_count)
    left, right = lax.rem(tile + tile_count - 1, tile_count), lax.rem(tile + 1, tile_count)
    rim_copies = [
        copy(leaving_ref.at[d], rims.at[(d + 2) % 4], rim_send.at[d], rim_recv.at[(d + 2) % 4], *to)
        for d, to in enumerate([(up, tile), (face, right), (down, tile), (face, left)])
    ]
    for one in sent + rim_copies:
        one.start()
    face_box[face] = sums_ref[rows_of(face, block)]
    face_extra[face] = sums_ref[channels : channels + 16]
    for k, to, source in faces:
        copy(
            face_box.at[source], face_box.at[source], face_send.at[k], face_recv.at[source], to, tile
        ).wait_recv()
        copy(
            face_extra.at[source],
            face_extra.at[source],
            face_xsend.at[k],
            face_xrecv.at[source],
            to,
            tile,
        ).wait_recv()
    acc, small = face_box[0], face_extra[0]
    for f in range(1, face_count):
        acc, small = acc + face_box[f], small + face_extra[f]
    part[...] = acc
    extra[...] = small

    for k, to, _ in tiles:

        @pl.when(to < owners)
        def _():
            copy(
                part.at[rows_of(to, piece)],
                tile_box.at[tile],
                tile_send.at[k],
                tile_recv.at[tile],
                face,
                to,
            ).start()

        one = copy(
            extra, tile_extra.at[tile], tile_xsend.at[k], tile_xrecv.at[tile], face, to
        )
        one.start()
        sent.append(one)
    tile_extra[tile] = extra[...]

    @pl.when(tile < owners)
    def _():
        tile_box[tile] = part[rows_of(tile, piece)]
        for k, to, source in tiles:
            copy(
                tile_box.at[source],
                tile_box.at[source],
                tile_send.at[k],
                tile_recv.at[source],
                face,
                to,
            ).wait_recv()
        acc = tile_box[0]
        for t in range(1, tile_count):
            acc = acc + tile_box[t]
        mine = rows_of(face * owners + tile, piece)
        total[mine] = acc
        for k, to, _ in tiles:
            copy(
                total.at[mine], total.at[mine], tile_gsend.at[k], tile_grecv.at[tile], face, to
            ).start()

    for k, to, source in tiles:

        @pl.when(source < owners)
        def _():
            theirs = rows_of(face * owners + source, piece)
            copy(
                total.at[theirs], total.at[theirs], tile_gsend.at[k], tile_grecv.at[source], face, to
            ).wait_recv()

    mine = rows_of(face, block)
    for k, to, _ in faces:
        one = copy(total.at[mine], total.at[mine], face_gsend.at[k], face_grecv.at[face], to, tile)
        one.start()
        sent.append(one)
    for k, to, source in tiles:
        copy(
            tile_extra.at[source],
            tile_extra.at[source],
            tile_xsend.at[k],
            tile_xrecv.at[source],
            face,
            to,
        ).wait_recv()
    small = tile_extra[0]
    for t in range(1, tile_count):
        small = small + tile_extra[t]
    depth_ref[...] = small[:9]
    bias_ref[...] = small[9:10]
    for one in rim_copies:
        one.wait_recv()
    returned_ref[...] = rims[...]
    for k, to, source in faces:
        theirs = rows_of(source, block)
        copy(
            total.at[theirs], total.at[theirs], face_gsend.at[k], face_grecv.at[source], to, tile
        ).wait_recv()
    point_ref[...] = total[...]
    for one in sent + rim_copies:
        one.wait_send()
    for k, to, _ in tiles:

        @pl.when(to < owners)
        def _():
            copy(
                part.at[rows_of(to, piece)],
                tile_box.at[tile],
                tile_send.at[k],
                tile_recv.at[tile],
                face,
                to,
            ).wait_send()

        @pl.when(tile < owners)
        def _():
            own = rows_of(face * owners + tile, piece)
            copy(
                total.at[own], total.at[own], tile_gsend.at[k], tile_grecv.at[tile], face, to
            ).wait_send()


def return_and_sum(leaving, sums):
    face_count, tile_count = lax.axis_size("face"), lax.axis_size("tile")
    channels = sums.shape[1]
    block = channels // face_count
    piece = block // min(tile_count, block // 8)
    vmem = pl.BlockSpec(memory_space=pltpu.VMEM)
    dma = pltpu.SemaphoreType.DMA
    return pl.pallas_call(
        functools.partial(comm_kernel, face_count, tile_count),
        in_specs=[vmem, vmem],
        out_specs=[vmem] * 4,
        out_shape=[
            jax.ShapeDtypeStruct(leaving.shape, BF16),
            jax.ShapeDtypeStruct((channels, channels), F32),
            jax.ShapeDtypeStruct((9, channels), F32),
            jax.ShapeDtypeStruct((1, channels), F32),
        ],
        scratch_shapes=[
            pltpu.VMEM(leaving.shape, BF16),
            pltpu.VMEM((face_count, block, channels), F32),
            pltpu.VMEM((face_count, 16, channels), F32),
            pltpu.VMEM((tile_count, piece, channels), F32),
            pltpu.VMEM((tile_count, 16, channels), F32),
            pltpu.VMEM((block, channels), F32),
            pltpu.VMEM((16, channels), F32),
            pltpu.VMEM((channels, channels), F32),
            dma((4,)),
            dma((4,)),
        ]
        + [dma((face_count,))] * 4
        + [dma((tile_count,))] * 6
        + [dma((face_count,))] * 2,
        compiler_params=pltpu.CompilerParams(
            collective_id=0, has_side_effects=True, vmem_limit_bytes=32 * 2**20
        ),
    )(leaving, sums)


def rim_terms(tap_rows, edges, mask_low, mask_high):
    length = edges.shape[2]
    spot = lax.broadcasted_iota(jnp.int32, (1, 1, length, 1), 2)
    padded_rows = jnp.pad(edges, ((0, 0), (0, 0), (1, 1), (0, 0)))
    tap_first = tap_rows[:, 0][:, None, None, :]
    tap_middle = tap_rows[:, 1][:, None, None, :]
    tap_last = tap_rows[:, 2][:, None, None, :]
    return (
        (tap_first * padded_rows[:, :, 2:] + tap_middle * edges)
        + tap_last * padded_rows[:, :, :-2]
        + jnp.where(spot == 0, (0.5 * mask_low) * tap_first * edges, 0.0)
        + jnp.where(spot == length - 1, (0.5 * mask_high) * tap_last * edges, 0.0)
    )


def shards(
    state_field,
    cotangent,
    depth_weight,
    depth_bias,
    point_weight,
    tile_links,
    link_sides,
    link_flips,
    corner_masks,
):
    batch, side, _, channels = state_field.shape
    face_count = lax.axis_size("face")
    tile_count = lax.axis_size("tile")
    face_pos = lax.axis_index("face")
    tile_pos = lax.axis_index("tile")
    toward = jnp.stack(
        [
            (face_pos - 1) % face_count * tile_count + tile_pos,
            face_pos * tile_count + (tile_pos + 1) % tile_count,
            (face_pos + 1) % face_count * tile_count + tile_pos,
            face_pos * tile_count + (tile_pos - 1) % tile_count,
        ]
    )
    matched = tile_links[0][:, None] == toward[None, :]
    counter = jnp.arange(4, dtype=jnp.int32)
    dir_of_side = jnp.sum(jnp.where(matched, counter[None, :], 0), axis=1)
    side_of_dir = jnp.sum(jnp.where(matched, counter[:, None], 0), axis=0)
    cmask = corner_masks[0].astype(F32)
    norm_scale = float(batch * side * side * face_count * tile_count) ** (-0.5)

    edges = jnp.stack(
        [state_field[:, 0], state_field[:, :, -1], state_field[:, -1], state_field[:, :, 0]]
    )
    rims = exchange(jnp.take(edges, side_of_dir, axis=0))
    links = jnp.stack([dir_of_side, link_flips[0], corner_masks[0]])

    whole = pl.BlockSpec((1, side, side, channels), lambda b, s: (b, 0, 0, 0))
    rows_of = pl.BlockSpec((1, ROWS, side, channels), lambda b, s: (b, s, 0, 0))
    line = pl.BlockSpec((1, side, 1, channels), lambda b, s: (b, 0, 0, 0))
    flat = pl.BlockSpec((1, side, channels), lambda b, s: (b, 0, 0))
    fixed = lambda *shape: pl.BlockSpec(shape, lambda b, s: (0,) * len(shape))
    pixels = batch * side * side
    sum_rows = channels + 16
    grad_hidden, grad_north, grad_south, grad_west, grad_east, sums = pl.pallas_call(
        functools.partial(first_kernel, norm_scale),
        grid=(batch, side // ROWS),
        in_specs=[
            whole,
            rows_of,
            pl.BlockSpec((4, 1, side, channels), lambda b, s: (0, b, 0, 0)),
            pl.BlockSpec(memory_space=pltpu.SMEM),
            fixed(9, channels),
            fixed(1, channels),
            fixed(channels, channels),
        ],
        out_specs=[rows_of, flat, flat, line, line, fixed(sum_rows, channels)],
        out_shape=[
            jax.ShapeDtypeStruct(state_field.shape, BF16),
            jax.ShapeDtypeStruct((batch, side, channels), F32),
            jax.ShapeDtypeStruct((batch, side, channels), F32),
            jax.ShapeDtypeStruct((batch, side, 1, channels), F32),
            jax.ShapeDtypeStruct((batch, side, 1, channels), F32),
            jax.ShapeDtypeStruct((sum_rows, channels), F32),
        ],
        scratch_shapes=[
            pltpu.VMEM((3, side + 2, side, channels), F32),
            pltpu.VMEM((ROWS, side, channels), F32),
            pltpu.VMEM((ROWS, side, channels), BF16),
            pltpu.VMEM((10, 8, channels), F32),
            pltpu.VMEM((side, 1, channels), F32),
            pltpu.VMEM((side, 1, channels), F32),
        ],
        compiler_params=pltpu.CompilerParams(vmem_limit_bytes=48 * 2**20),
        cost_estimate=pl.CostEstimate(
            flops=4 * pixels * channels * channels,
            bytes_accessed=6 * pixels * channels,
            transcendentals=pixels * channels,
        ),
    )(
        state_field,
        cotangent,
        rims,
        links,
        depth_weight,
        depth_bias[None],
        point_weight,
    )

    tap_table = depth_weight.reshape(3, 3, channels)
    side_taps = jnp.stack([tap_table[0], tap_table[:, 2], tap_table[2], tap_table[:, 0]], axis=0)
    mask_low = cmask[jnp.array([0, 1, 3, 0])][:, None, None, None]
    mask_high = cmask[jnp.array([1, 2, 2, 3])][:, None, None, None]
    grad_edges = jnp.stack(
        [
            grad_north,
            grad_east[:, :, 0],
            grad_south,
            grad_west[:, :, 0],
        ]
    )
    leaving = rim_terms(side_taps, grad_edges, mask_low, mask_high).astype(BF16)
    leaving = jnp.take(leaving, side_of_dir, axis=0)
    returned, point_sum, depth_sum, bias_sum = return_and_sum(
        leaving.reshape(4, batch * side, channels), sums
    )

    whole = pl.BlockSpec((1, side, side, channels), lambda b: (b, 0, 0, 0))
    field_grad = pl.pallas_call(
        second_kernel,
        grid=(batch,),
        in_specs=[
            whole,
            pl.BlockSpec((4, 1, side, channels), lambda b: (0, b, 0, 0)),
            pl.BlockSpec(memory_space=pltpu.SMEM),
            pl.BlockSpec((9, channels), lambda b: (0, 0)),
        ],
        out_specs=whole,
        scratch_shapes=[
            pltpu.VMEM((side, channels), F32),
            pltpu.VMEM((side, channels), F32),
            pltpu.VMEM((side, 1, channels), F32),
            pltpu.VMEM((side, 1, channels), F32),
        ],
        out_shape=jax.ShapeDtypeStruct(state_field.shape, BF16),
        compiler_params=pltpu.CompilerParams(vmem_limit_bytes=48 * 2**20),
        cost_estimate=pl.CostEstimate(
            flops=40 * pixels * channels,
            bytes_accessed=4 * pixels * channels,
            transcendentals=0,
        ),
    )(
        grad_hidden,
        returned.reshape(leaving.shape),
        links,
        depth_weight,
    )
    return field_grad, depth_sum, bias_sum[0], point_sum


def solution(mesh):
    in_specs = (
        P(None, "face", "tile", None),
        P(None, "face", "tile", None),
        P(),
        P(),
        P(),
        P(("face", "tile"), None),
        P(("face", "tile"), None),
        P(("face", "tile"), None),
        P(("face", "tile"), None),
    )
    out_specs = (P(None, "face", "tile", None), P(), P(), P())
    return jax.shard_map(shards, mesh=mesh, in_specs=in_specs, out_specs=out_specs, check_vma=False)
```

```python
import functools

import jax
import jax.numpy as jnp
from jax import lax
from jax.experimental import pallas as pl
from jax.experimental.pallas import tpu as pltpu
from jax.sharding import PartitionSpec as P

root_two_pi = 0.7978845608028654
cubic_coef = 0.044715
HALF = 128
STRIP = 16
ROWS = 16
F32 = jnp.float32
BF16 = jnp.bfloat16


def gelu_pair(hidden):
    square = hidden * hidden
    gate = 0.5 + 0.5 * jnp.tanh(hidden * (root_two_pi + (root_two_pi * cubic_coef) * square))
    output = hidden * gate
    slope = gate + output * (1.0 - gate) * (
        2.0 * root_two_pi + (6.0 * root_two_pi * cubic_coef) * square
    )
    return output, slope


def rim_of_side(by_dir_ref, links_ref, s):
    rows = by_dir_ref[links_ref[0, s], 0]
    side = rows.shape[0]
    spots = [lax.broadcasted_iota(jnp.int32, (side, side), axis) for axis in range(2)]
    swap = jnp.where(spots[0] + spots[1] == side - 1, 1.0, 0.0).astype(BF16)
    turned = jnp.dot(swap, rows, preferred_element_type=F32)
    return jnp.where(jnp.full(rows.shape, links_ref[1, s]) == 1, turned, rows.astype(F32))


def into_lines(lines_ref, rows):
    for i in range(rows.shape[0]):
        lines_ref[i] = rows[i : i + 1]


def first_kernel(
    norm_scale,
    x_ref,
    cot_ref,
    rims_ref,
    links_ref,
    taps_ref,
    bias_ref,
    point_ref,
    g_ref,
    leaving_ref,
    sums_ref,
    win,
    grad_act,
    act,
    parts,
    west,
    east,
    gwest,
    geast,
    gedges,
):
    sample, step = pl.program_id(0), pl.program_id(1)
    side, channels = x_ref.shape[1], x_ref.shape[3]
    rows = cot_ref.shape[1]

    @pl.when(step == 0)
    def _():
        rims = [rim_of_side(rims_ref, links_ref, s) for s in range(4)]
        into_lines(west, rims[3])
        into_lines(east, rims[1])

        def corner(c, one, other):
            mask = jnp.full((1, channels), links_ref[2, c]).astype(F32)
            return (mask * 0.5 * (one + other)).astype(BF16).astype(F32)

        north_west = corner(0, rims[0][:1], rims[3][:1])
        north_east = corner(1, rims[0][side - 1 :], rims[1][:1])
        south_east = corner(2, rims[1][side - 1 :], rims[2][side - 1 :])
        south_west = corner(3, rims[2][:1], rims[3][side - 1 :])
        spot = lax.broadcasted_iota(jnp.int32, (side, channels), 0)
        for at, rim, low, high in (
            (0, rims[0], north_west, north_east),
            (side + 1, rims[2], south_west, south_east),
        ):
            win[0, at] = jnp.where(spot == 0, low, pltpu.roll(rim, 1, 0))
            win[1, at] = rim
            win[2, at] = jnp.where(spot == side - 1, high, pltpu.roll(rim, side - 1, 0))
        spot = lax.broadcasted_iota(jnp.int32, (side, HALF), 0)
        for lane in range(0, channels, HALF):
            lanes = pl.ds(lane, HALF)

            def shift(i, carry):
                mid = x_ref[0, i, :, lanes].astype(F32)
                win[1, i + 1, :, lanes] = mid
                win[0, i + 1, :, lanes] = jnp.where(
                    spot == 0, west[i, :, lanes], pltpu.roll(mid, 1, 0)
                )
                win[2, i + 1, :, lanes] = jnp.where(
                    spot == side - 1, east[i, :, lanes], pltpu.roll(mid, side - 1, 0)
                )
                return carry

            lax.fori_loop(0, side, shift, 0, unroll=2)

    @pl.when((step == 0) & (sample == 0))
    def _():
        sums_ref[...] = jnp.zeros_like(sums_ref)
        parts[...] = jnp.zeros_like(parts)

    cot = cot_ref[0].reshape(rows * side, channels)
    grad_act[...] = lax.dot_general(
        cot, point_ref[...], (((1,), (1,)), ((), ())), preferred_element_type=F32
    ).reshape(rows, side, channels)
    for lane in range(0, channels, HALF):
        lanes = pl.ds(lane, HALF)

        def row(k, held):
            held = list(held)
            i = step * rows + k
            for low in range(0, side, STRIP):
                spots = pl.ds(low, STRIP)
                views = [
                    win[col_off, i + row_off, spots, lanes]
                    for row_off in range(3)
                    for col_off in range(3)
                ]
                hidden = bias_ref[0:1, lanes] + taps_ref[0:1, lanes] * views[0]
                for t in range(1, 9):
                    hidden = hidden + taps_ref[t : t + 1, lanes] * views[t]
                output, slope = gelu_pair(hidden)
                act[k, spots, lanes] = output.astype(BF16)
                grad = (grad_act[k, spots, lanes] * slope).astype(BF16)
                g_ref[0, k, spots, lanes] = grad
                grad = grad.astype(F32)
                if low == 0:
                    gwest[i, :, lanes] = grad[:1]
                if low + STRIP == side:
                    geast[i, :, lanes] = grad[STRIP - 1 :]
                for t in range(9):
                    term = grad * views[t]
                    held[t] = held[t] + (term[:8] + term[8:])
                held[9] = held[9] + (grad[:8] + grad[8:])
            return tuple(held)

        held = lax.fori_loop(0, rows, row, tuple(parts[t, :, lanes] for t in range(10)))
        for t in range(10):
            parts[t, :, lanes] = held[t]
    sums_ref[0:channels] += lax.dot_general(
        act[...].reshape(rows * side, channels),
        cot,
        (((0,), (0,)), ((), ())),
        preferred_element_type=F32,
    )

    @pl.when(step == 0)
    def _():
        gedges[0] = g_ref[0, 0].astype(F32)

    @pl.when(step == pl.num_programs(1) - 1)
    def _():
        gedges[2] = g_ref[0, rows - 1].astype(F32)
        for i in range(side):
            gedges[1, i : i + 1] = geast[i]
            gedges[3, i : i + 1] = gwest[i]
        spot = lax.broadcasted_iota(jnp.int32, (side, channels), 0)
        for s, (first, middle, last, low, high) in enumerate(
            [(0, 1, 2, 0, 1), (2, 5, 8, 1, 2), (6, 7, 8, 3, 2), (0, 3, 6, 0, 3)]
        ):
            edge = gedges[s]
            share = [
                0.5 * jnp.full((1, channels), links_ref[2, c]).astype(F32) for c in (low, high)
            ]
            onward = taps_ref[first : first + 1, :] * jnp.where(
                spot == side - 1, 0.0, pltpu.roll(edge, side - 1, 0)
            )
            back = taps_ref[last : last + 1, :] * jnp.where(spot == 0, 0.0, pltpu.roll(edge, 1, 0))
            ends = jnp.where(spot == 0, share[0] * taps_ref[first : first + 1, :] * edge, 0.0)
            ends = ends + jnp.where(
                spot == side - 1, share[1] * taps_ref[last : last + 1, :] * edge, 0.0
            )
            rim = onward + taps_ref[middle : middle + 1, :] * edge + back + ends
            leaving_ref[links_ref[0, s], 0] = rim.astype(BF16)

    @pl.when((step == pl.num_programs(1) - 1) & (sample == pl.num_programs(0) - 1))
    def _():
        for t in range(10):
            sums_ref[channels + t : channels + t + 1] = jnp.sum(parts[t], axis=0, keepdims=True)
        sums_ref[...] = sums_ref[...] * norm_scale


def second_kernel(g_ref, rims_ref, links_ref, taps_ref, out_ref, north, south, west, east):
    side, channels = g_ref.shape[1], g_ref.shape[3]
    north[...] = rim_of_side(rims_ref, links_ref, 0)
    into_lines(east, rim_of_side(rims_ref, links_ref, 1))
    south[...] = rim_of_side(rims_ref, links_ref, 2)
    into_lines(west, rim_of_side(rims_ref, links_ref, 3))
    spot = lax.broadcasted_iota(jnp.int32, (side, HALF), 0)
    for lane in range(0, channels, HALF):
        lanes = pl.ds(lane, HALF)

        def mixed(i, before, here, after):
            cols = [
                taps_ref[c : c + 1, lanes] * after
                + taps_ref[3 + c : 4 + c, lanes] * here
                + taps_ref[6 + c : 7 + c, lanes] * before
                for c in range(3)
            ]
            from_right = jnp.where(
                spot == side - 1, east[i, :, lanes], pltpu.roll(cols[0], side - 1, 0)
            )
            from_left = jnp.where(
                spot == 0, west[i, :, lanes], pltpu.roll(cols[2], 1, 0)
            )
            return cols[1] + from_right + from_left

        def load(i):
            return g_ref[0, i, :, lanes].astype(F32)

        empty = jnp.zeros((side, HALF), F32)
        first, second = load(0), load(1)
        out_ref[0, 0, :, lanes] = (
            mixed(0, empty, first, second) + north[:, lanes]
        ).astype(BF16)

        def row(i, held):
            after = load(i + 1)
            out_ref[0, i, :, lanes] = mixed(i, held[0], held[1], after).astype(BF16)
            return held[1], after

        before, here = lax.fori_loop(1, side - 1, row, (first, second))
        out_ref[0, side - 1, :, lanes] = (
            mixed(side - 1, before, here, empty) + south[:, lanes]
        ).astype(BF16)


def exchange(by_dir):
    face_count, tile_count = lax.axis_size("face"), lax.axis_size("tile")
    up = [(i, (i + 1) % face_count) for i in range(face_count)]
    right = [(i, (i + 1) % tile_count) for i in range(tile_count)]
    down = [(b, a) for a, b in up]
    left = [(b, a) for a, b in right]
    return jnp.stack(
        [
            lax.ppermute(by_dir[2], "face", up),
            lax.ppermute(by_dir[3], "tile", left),
            lax.ppermute(by_dir[0], "face", down),
            lax.ppermute(by_dir[1], "tile", right),
        ]
    )


def comm_kernel(
    face_count,
    tile_count,
    leaving_ref,
    sums_ref,
    returned_ref,
    point_ref,
    depth_ref,
    bias_ref,
    rims,
    face_box,
    face_extra,
    tile_box,
    tile_extra,
    part,
    extra,
    total,
    rim_send,
    rim_recv,
    face_send,
    face_recv,
    face_xsend,
    face_xrecv,
    tile_send,
    tile_recv,
    tile_xsend,
    tile_xrecv,
    tile_gsend,
    tile_grecv,
    face_gsend,
    face_grecv,
):
    face, tile = lax.axis_index("face"), lax.axis_index("tile")
    channels = point_ref.shape[0]
    block = channels // face_count
    owners = min(tile_count, block // 8)
    piece = block // owners

    def copy(src, dst, send_sem, recv_sem, to_face, to_tile):
        return pltpu.make_async_remote_copy(
            src_ref=src,
            dst_ref=dst,
            send_sem=send_sem,
            recv_sem=recv_sem,
            device_id=(to_face, to_tile),
            device_id_type=pl.DeviceIdType.MESH,
        )

    faces = [
        (k, lax.rem(face + k, face_count), lax.rem(face + face_count - k, face_count))
        for k in range(1, face_count)
    ]
    tiles = [
        (k, lax.rem(tile + k, tile_count), lax.rem(tile + tile_count - k, tile_count))
        for k in range(1, tile_count)
    ]

    barrier = pltpu.get_barrier_semaphore()
    for _, to, _ in faces:
        pl.semaphore_signal(
            barrier, inc=1, device_id=(to, tile), device_id_type=pl.DeviceIdType.MESH
        )
    for _, to, _ in tiles:
        pl.semaphore_signal(
            barrier, inc=1, device_id=(face, to), device_id_type=pl.DeviceIdType.MESH
        )
    pl.semaphore_wait(barrier, face_count + tile_count - 2)

    def rows_of(index, size):
        return pl.ds(pl.multiple_of(index * size, 8), size)

    sent = []
    for k, to, _ in faces:
        sent.append(
            copy(
                sums_ref.at[rows_of(to, block)],
                face_box.at[face],
                face_send.at[k],
                face_recv.at[face],
                to,
                tile,
            )
        )
        sent.append(
            copy(
                sums_ref.at[pl.ds(channels, 16)],
                face_extra.at[face],
                face_xsend.at[k],
                face_xrecv.at[face],
                to,
                tile,
            )
        )
    up, down = lax.rem(face + face_count - 1, face_count), lax.rem(face + 1, face_count)
    left, right = lax.rem(tile + tile_count - 1, tile_count), lax.rem(tile + 1, tile_count)
    rim_copies = [
        copy(leaving_ref.at[d], rims.at[(d + 2) % 4], rim_send.at[d], rim_recv.at[(d + 2) % 4], *to)
        for d, to in enumerate([(up, tile), (face, right), (down, tile), (face, left)])
    ]
    for one in sent + rim_copies:
        one.start()
    face_box[face] = sums_ref[rows_of(face, block)]
    face_extra[face] = sums_ref[channels : channels + 16]
    for k, to, source in faces:
        copy(
            face_box.at[source], face_box.at[source], face_send.at[k], face_recv.at[source], to, tile
        ).wait_recv()
        copy(
            face_extra.at[source],
            face_extra.at[source],
            face_xsend.at[k],
            face_xrecv.at[source],
            to,
            tile,
        ).wait_recv()
    acc, small = face_box[0], face_extra[0]
    for f in range(1, face_count):
        acc, small = acc + face_box[f], small + face_extra[f]
    part[...] = acc
    extra[...] = small

    for k, to, _ in tiles:

        @pl.when(to < owners)
        def _():
            copy(
                part.at[rows_of(to, piece)],
                tile_box.at[tile],
                tile_send.at[k],
                tile_recv.at[tile],
                face,
                to,
            ).start()

        one = copy(
            extra, tile_extra.at[tile], tile_xsend.at[k], tile_xrecv.at[tile], face, to
        )
        one.start()
        sent.append(one)
    tile_extra[tile] = extra[...]

    @pl.when(tile < owners)
    def _():
        tile_box[tile] = part[rows_of(tile, piece)]
        for k, to, source in tiles:
            copy(
                tile_box.at[source],
                tile_box.at[source],
                tile_send.at[k],
                tile_recv.at[source],
                face,
                to,
            ).wait_recv()
        acc = tile_box[0]
        for t in range(1, tile_count):
            acc = acc + tile_box[t]
        mine = rows_of(face * owners + tile, piece)
        total[mine] = acc
        for k, to, _ in tiles:
            copy(
                total.at[mine], total.at[mine], tile_gsend.at[k], tile_grecv.at[tile], face, to
            ).start()

    for k, to, source in tiles:

        @pl.when(source < owners)
        def _():
            theirs = rows_of(face * owners + source, piece)
            copy(
                total.at[theirs], total.at[theirs], tile_gsend.at[k], tile_grecv.at[source], face, to
            ).wait_recv()

    mine = rows_of(face, block)
    for k, to, _ in faces:
        one = copy(total.at[mine], total.at[mine], face_gsend.at[k], face_grecv.at[face], to, tile)
        one.start()
        sent.append(one)
    for k, to, source in tiles:
        copy(
            tile_extra.at[source],
            tile_extra.at[source],
            tile_xsend.at[k],
            tile_xrecv.at[source],
            face,
            to,
        ).wait_recv()
    small = tile_extra[0]
    for t in range(1, tile_count):
        small = small + tile_extra[t]
    depth_ref[...] = small[:9]
    bias_ref[...] = small[9:10]
    for one in rim_copies:
        one.wait_recv()
    returned_ref[...] = rims[...]
    for k, to, source in faces:
        theirs = rows_of(source, block)
        copy(
            total.at[theirs], total.at[theirs], face_gsend.at[k], face_grecv.at[source], to, tile
        ).wait_recv()
    point_ref[...] = total[...]
    for one in sent + rim_copies:
        one.wait_send()
    for k, to, _ in tiles:

        @pl.when(to < owners)
        def _():
            copy(
                part.at[rows_of(to, piece)],
                tile_box.at[tile],
                tile_send.at[k],
                tile_recv.at[tile],
                face,
                to,
            ).wait_send()

        @pl.when(tile < owners)
        def _():
            own = rows_of(face * owners + tile, piece)
            copy(
                total.at[own], total.at[own], tile_gsend.at[k], tile_grecv.at[tile], face, to
            ).wait_send()


def return_and_sum(leaving, sums):
    face_count, tile_count = lax.axis_size("face"), lax.axis_size("tile")
    channels = sums.shape[1]
    block = channels // face_count
    piece = block // min(tile_count, block // 8)
    vmem = pl.BlockSpec(memory_space=pltpu.VMEM)
    dma = pltpu.SemaphoreType.DMA
    return pl.pallas_call(
        functools.partial(comm_kernel, face_count, tile_count),
        in_specs=[vmem, vmem],
        out_specs=[vmem] * 4,
        out_shape=[
            jax.ShapeDtypeStruct(leaving.shape, BF16),
            jax.ShapeDtypeStruct((channels, channels), F32),
            jax.ShapeDtypeStruct((9, channels), F32),
            jax.ShapeDtypeStruct((1, channels), F32),
        ],
        scratch_shapes=[
            pltpu.VMEM(leaving.shape, BF16),
            pltpu.VMEM((face_count, block, channels), F32),
            pltpu.VMEM((face_count, 16, channels), F32),
            pltpu.VMEM((tile_count, piece, channels), F32),
            pltpu.VMEM((tile_count, 16, channels), F32),
            pltpu.VMEM((block, channels), F32),
            pltpu.VMEM((16, channels), F32),
            pltpu.VMEM((channels, channels), F32),
            dma((4,)),
            dma((4,)),
        ]
        + [dma((face_count,))] * 4
        + [dma((tile_count,))] * 6
        + [dma((face_count,))] * 2,
        compiler_params=pltpu.CompilerParams(
            collective_id=0, has_side_effects=True, vmem_limit_bytes=32 * 2**20
        ),
    )(leaving, sums)


def shards(
    state_field,
    cotangent,
    depth_weight,
    depth_bias,
    point_weight,
    tile_links,
    link_sides,
    link_flips,
    corner_masks,
):
    batch, side, _, channels = state_field.shape
    face_count = lax.axis_size("face")
    tile_count = lax.axis_size("tile")
    face_pos = lax.axis_index("face")
    tile_pos = lax.axis_index("tile")
    toward = jnp.stack(
        [
            (face_pos - 1) % face_count * tile_count + tile_pos,
            face_pos * tile_count + (tile_pos + 1) % tile_count,
            (face_pos + 1) % face_count * tile_count + tile_pos,
            face_pos * tile_count + (tile_pos - 1) % tile_count,
        ]
    )
    matched = tile_links[0][:, None] == toward[None, :]
    counter = jnp.arange(4, dtype=jnp.int32)
    dir_of_side = jnp.sum(jnp.where(matched, counter[None, :], 0), axis=1)
    side_of_dir = jnp.sum(jnp.where(matched, counter[:, None], 0), axis=0)
    norm_scale = float(batch * side * side * face_count * tile_count) ** (-0.5)

    edges = jnp.stack(
        [state_field[:, 0], state_field[:, :, -1], state_field[:, -1], state_field[:, :, 0]]
    )
    rims = exchange(jnp.take(edges, side_of_dir, axis=0))
    links = jnp.stack([dir_of_side, link_flips[0], corner_masks[0]])

    whole = pl.BlockSpec((1, side, side, channels), lambda b, s: (b, 0, 0, 0))
    rows_of = pl.BlockSpec((1, ROWS, side, channels), lambda b, s: (b, s, 0, 0))
    fixed = lambda *shape: pl.BlockSpec(shape, lambda b, s: (0,) * len(shape))
    pixels = batch * side * side
    sum_rows = channels + 16
    grad_hidden, leaving, sums = pl.pallas_call(
        functools.partial(first_kernel, norm_scale),
        grid=(batch, side // ROWS),
        in_specs=[
            whole,
            rows_of,
            pl.BlockSpec((4, 1, side, channels), lambda b, s: (0, b, 0, 0)),
            pl.BlockSpec(memory_space=pltpu.SMEM),
            fixed(9, channels),
            fixed(1, channels),
            fixed(channels, channels),
        ],
        out_specs=[
            rows_of,
            pl.BlockSpec((4, 1, side, channels), lambda b, s: (0, b, 0, 0)),
            fixed(sum_rows, channels),
        ],
        out_shape=[
            jax.ShapeDtypeStruct(state_field.shape, BF16),
            jax.ShapeDtypeStruct((4, batch, side, channels), BF16),
            jax.ShapeDtypeStruct((sum_rows, channels), F32),
        ],
        scratch_shapes=[
            pltpu.VMEM((3, side + 2, side, channels), F32),
            pltpu.VMEM((ROWS, side, channels), F32),
            pltpu.VMEM((ROWS, side, channels), BF16),
            pltpu.VMEM((10, 8, channels), F32),
        ]
        + [pltpu.VMEM((side, 1, channels), F32)] * 4
        + [pltpu.VMEM((4, side, channels), F32)],
        compiler_params=pltpu.CompilerParams(vmem_limit_bytes=48 * 2**20),
        cost_estimate=pl.CostEstimate(
            flops=4 * pixels * channels * channels,
            bytes_accessed=6 * pixels * channels,
            transcendentals=pixels * channels,
        ),
    )(
        state_field,
        cotangent,
        rims,
        links,
        depth_weight,
        depth_bias[None],
        point_weight,
    )

    returned, point_sum, depth_sum, bias_sum = return_and_sum(
        leaving.reshape(4, batch * side, channels), sums
    )

    whole = pl.BlockSpec((1, side, side, channels), lambda b: (b, 0, 0, 0))
    field_grad = pl.pallas_call(
        second_kernel,
        grid=(batch,),
        in_specs=[
            whole,
            pl.BlockSpec((4, 1, side, channels), lambda b: (0, b, 0, 0)),
            pl.BlockSpec(memory_space=pltpu.SMEM),
            pl.BlockSpec((9, channels), lambda b: (0, 0)),
        ],
        out_specs=whole,
        scratch_shapes=[
            pltpu.VMEM((side, channels), F32),
            pltpu.VMEM((side, channels), F32),
            pltpu.VMEM((side, 1, channels), F32),
            pltpu.VMEM((side, 1, channels), F32),
        ],
        out_shape=jax.ShapeDtypeStruct(state_field.shape, BF16),
        compiler_params=pltpu.CompilerParams(vmem_limit_bytes=48 * 2**20),
        cost_estimate=pl.CostEstimate(
            flops=40 * pixels * channels,
            bytes_accessed=4 * pixels * channels,
            transcendentals=0,
        ),
    )(
        grad_hidden,
        returned.reshape(leaving.shape),
        links,
        depth_weight,
    )
    return field_grad, depth_sum, bias_sum[0], point_sum


def solution(mesh):
    in_specs = (
        P(None, "face", "tile", None),
        P(None, "face", "tile", None),
        P(),
        P(),
        P(),
        P(("face", "tile"), None),
        P(("face", "tile"), None),
        P(("face", "tile"), None),
        P(("face", "tile"), None),
    )
    out_specs = (P(None, "face", "tile", None), P(), P(), P())
    return jax.shard_map(shards, mesh=mesh, in_specs=in_specs, out_specs=out_specs, check_vma=False)
```

```python
import functools

import jax
import jax.numpy as jnp
from jax import lax
from jax.experimental import pallas as pl
from jax.experimental.pallas import tpu as pltpu
from jax.sharding import PartitionSpec as P

root_two_pi = 0.7978845608028654
cubic_coef = 0.044715
HALF = 128
STRIP = 16
ROWS = 32
F32 = jnp.float32
BF16 = jnp.bfloat16


def gelu_pair(hidden):
    square = hidden * hidden
    gate = 0.5 + 0.5 * jnp.tanh(hidden * (root_two_pi + (root_two_pi * cubic_coef) * square))
    output = hidden * gate
    slope = gate + output * (1.0 - gate) * (
        2.0 * root_two_pi + (6.0 * root_two_pi * cubic_coef) * square
    )
    return output, slope


def rim_of_side(by_dir_ref, links_ref, s):
    rows = by_dir_ref[links_ref[0, s], 0]
    side = rows.shape[0]
    spots = [lax.broadcasted_iota(jnp.int32, (side, side), axis) for axis in range(2)]
    swap = jnp.where(spots[0] + spots[1] == side - 1, 1.0, 0.0).astype(BF16)
    turned = jnp.dot(swap, rows, preferred_element_type=F32)
    return jnp.where(jnp.full(rows.shape, links_ref[1, s]) == 1, turned, rows.astype(F32))


def into_lines(lines_ref, rows):
    for i in range(rows.shape[0]):
        lines_ref[i] = rows[i : i + 1]


def first_kernel(
    norm_scale,
    x_ref,
    cot_ref,
    rims_ref,
    links_ref,
    taps_ref,
    bias_ref,
    point_ref,
    g_ref,
    leaving_ref,
    sums_ref,
    win,
    grad_act,
    act,
    parts,
    west,
    east,
    gwest,
    geast,
    gedges,
):
    sample, step = pl.program_id(0), pl.program_id(1)
    side, channels = x_ref.shape[1], x_ref.shape[3]
    rows = cot_ref.shape[1]

    @pl.when(step == 0)
    def _():
        rims = [rim_of_side(rims_ref, links_ref, s) for s in range(4)]
        into_lines(west, rims[3])
        into_lines(east, rims[1])

        def corner(c, one, other):
            mask = jnp.full((1, channels), links_ref[2, c]).astype(F32)
            return (mask * 0.5 * (one + other)).astype(BF16).astype(F32)

        north_west = corner(0, rims[0][:1], rims[3][:1])
        north_east = corner(1, rims[0][side - 1 :], rims[1][:1])
        south_east = corner(2, rims[1][side - 1 :], rims[2][side - 1 :])
        south_west = corner(3, rims[2][:1], rims[3][side - 1 :])
        spot = lax.broadcasted_iota(jnp.int32, (side, channels), 0)
        for at, rim, low, high in (
            (0, rims[0], north_west, north_east),
            (side + 1, rims[2], south_west, south_east),
        ):
            win[0, at] = jnp.where(spot == 0, low, pltpu.roll(rim, 1, 0))
            win[1, at] = rim
            win[2, at] = jnp.where(spot == side - 1, high, pltpu.roll(rim, side - 1, 0))
        spot = lax.broadcasted_iota(jnp.int32, (side, HALF), 0)
        for lane in range(0, channels, HALF):
            lanes = pl.ds(lane, HALF)

            def shift(i, carry):
                mid = x_ref[0, i, :, lanes].astype(F32)
                win[1, i + 1, :, lanes] = mid
                win[0, i + 1, :, lanes] = jnp.where(
                    spot == 0, west[i, :, lanes], pltpu.roll(mid, 1, 0)
                )
                win[2, i + 1, :, lanes] = jnp.where(
                    spot == side - 1, east[i, :, lanes], pltpu.roll(mid, side - 1, 0)
                )
                return carry

            lax.fori_loop(0, side, shift, 0, unroll=2)

    @pl.when((step == 0) & (sample == 0))
    def _():
        sums_ref[...] = jnp.zeros_like(sums_ref)
        parts[...] = jnp.zeros_like(parts)

    cot = cot_ref[0].reshape(rows * side, channels)
    grad_act[...] = lax.dot_general(
        cot, point_ref[...], (((1,), (1,)), ((), ())), preferred_element_type=F32
    ).reshape(rows, side, channels)
    for lane in range(0, channels, HALF):
        lanes = pl.ds(lane, HALF)

        def row(k, held):
            held = list(held)
            i = step * rows + k
            for low in range(0, side, STRIP):
                spots = pl.ds(low, STRIP)
                views = [
                    win[col_off, i + row_off, spots, lanes]
                    for row_off in range(3)
                    for col_off in range(3)
                ]
                hidden = bias_ref[0:1, lanes] + taps_ref[0:1, lanes] * views[0]
                for t in range(1, 9):
                    hidden = hidden + taps_ref[t : t + 1, lanes] * views[t]
                output, slope = gelu_pair(hidden)
                act[k, spots, lanes] = output.astype(BF16)
                grad = (grad_act[k, spots, lanes] * slope).astype(BF16)
                g_ref[0, k, spots, lanes] = grad
                grad = grad.astype(F32)
                if low == 0:
                    gwest[i, :, lanes] = grad[:1]
                if low + STRIP == side:
                    geast[i, :, lanes] = grad[STRIP - 1 :]
                for t in range(9):
                    term = grad * views[t]
                    held[t] = held[t] + (term[:8] + term[8:])
                held[9] = held[9] + (grad[:8] + grad[8:])
            return tuple(held)

        held = lax.fori_loop(0, rows, row, tuple(parts[t, :, lanes] for t in range(10)))
        for t in range(10):
            parts[t, :, lanes] = held[t]
    sums_ref[0:channels] += lax.dot_general(
        act[...].reshape(rows * side, channels),
        cot,
        (((0,), (0,)), ((), ())),
        preferred_element_type=F32,
    )

    @pl.when(step == 0)
    def _():
        gedges[0] = g_ref[0, 0].astype(F32)

    @pl.when(step == pl.num_programs(1) - 1)
    def _():
        gedges[2] = g_ref[0, rows - 1].astype(F32)
        for i in range(side):
            gedges[1, i : i + 1] = geast[i]
            gedges[3, i : i + 1] = gwest[i]
        spot = lax.broadcasted_iota(jnp.int32, (side, channels), 0)
        for s, (first, middle, last, low, high) in enumerate(
            [(0, 1, 2, 0, 1), (2, 5, 8, 1, 2), (6, 7, 8, 3, 2), (0, 3, 6, 0, 3)]
        ):
            edge = gedges[s]
            share = [
                0.5 * jnp.full((1, channels), links_ref[2, c]).astype(F32) for c in (low, high)
            ]
            onward = taps_ref[first : first + 1, :] * jnp.where(
                spot == side - 1, 0.0, pltpu.roll(edge, side - 1, 0)
            )
            back = taps_ref[last : last + 1, :] * jnp.where(spot == 0, 0.0, pltpu.roll(edge, 1, 0))
            ends = jnp.where(spot == 0, share[0] * taps_ref[first : first + 1, :] * edge, 0.0)
            ends = ends + jnp.where(
                spot == side - 1, share[1] * taps_ref[last : last + 1, :] * edge, 0.0
            )
            rim = onward + taps_ref[middle : middle + 1, :] * edge + back + ends
            leaving_ref[links_ref[0, s], 0] = rim.astype(BF16)

    @pl.when((step == pl.num_programs(1) - 1) & (sample == pl.num_programs(0) - 1))
    def _():
        for t in range(10):
            sums_ref[channels + t : channels + t + 1] = jnp.sum(parts[t], axis=0, keepdims=True)
        sums_ref[...] = sums_ref[...] * norm_scale


def second_kernel(g_ref, rims_ref, links_ref, taps_ref, out_ref, north, south, west, east):
    side, channels = g_ref.shape[1], g_ref.shape[3]
    north[...] = rim_of_side(rims_ref, links_ref, 0)
    into_lines(east, rim_of_side(rims_ref, links_ref, 1))
    south[...] = rim_of_side(rims_ref, links_ref, 2)
    into_lines(west, rim_of_side(rims_ref, links_ref, 3))
    spot = lax.broadcasted_iota(jnp.int32, (side, HALF), 0)
    for lane in range(0, channels, HALF):
        lanes = pl.ds(lane, HALF)

        def mixed(i, before, here, after):
            cols = [
                taps_ref[c : c + 1, lanes] * after
                + taps_ref[3 + c : 4 + c, lanes] * here
                + taps_ref[6 + c : 7 + c, lanes] * before
                for c in range(3)
            ]
            from_right = jnp.where(
                spot == side - 1, east[i, :, lanes], pltpu.roll(cols[0], side - 1, 0)
            )
            from_left = jnp.where(
                spot == 0, west[i, :, lanes], pltpu.roll(cols[2], 1, 0)
            )
            return cols[1] + from_right + from_left

        def load(i):
            return g_ref[0, i, :, lanes].astype(F32)

        empty = jnp.zeros((side, HALF), F32)
        first, second = load(0), load(1)
        out_ref[0, 0, :, lanes] = (
            mixed(0, empty, first, second) + north[:, lanes]
        ).astype(BF16)

        def row(i, held):
            after = load(i + 1)
            out_ref[0, i, :, lanes] = mixed(i, held[0], held[1], after).astype(BF16)
            return held[1], after

        before, here = lax.fori_loop(1, side - 1, row, (first, second))
        out_ref[0, side - 1, :, lanes] = (
            mixed(side - 1, before, here, empty) + south[:, lanes]
        ).astype(BF16)


def exchange(by_dir):
    face_count, tile_count = lax.axis_size("face"), lax.axis_size("tile")
    up = [(i, (i + 1) % face_count) for i in range(face_count)]
    right = [(i, (i + 1) % tile_count) for i in range(tile_count)]
    down = [(b, a) for a, b in up]
    left = [(b, a) for a, b in right]
    return jnp.stack(
        [
            lax.ppermute(by_dir[2], "face", up),
            lax.ppermute(by_dir[3], "tile", left),
            lax.ppermute(by_dir[0], "face", down),
            lax.ppermute(by_dir[1], "tile", right),
        ]
    )


def comm_kernel(
    face_count,
    tile_count,
    leaving_ref,
    sums_ref,
    returned_ref,
    point_ref,
    depth_ref,
    bias_ref,
    rims,
    face_box,
    face_extra,
    tile_box,
    tile_extra,
    part,
    extra,
    total,
    rim_send,
    rim_recv,
    face_send,
    face_recv,
    face_xsend,
    face_xrecv,
    tile_send,
    tile_recv,
    tile_xsend,
    tile_xrecv,
    tile_gsend,
    tile_grecv,
    face_gsend,
    face_grecv,
):
    face, tile = lax.axis_index("face"), lax.axis_index("tile")
    channels = point_ref.shape[0]
    block = channels // face_count
    owners = min(tile_count, block // 8)
    piece = block // owners

    def copy(src, dst, send_sem, recv_sem, to_face, to_tile):
        return pltpu.make_async_remote_copy(
            src_ref=src,
            dst_ref=dst,
            send_sem=send_sem,
            recv_sem=recv_sem,
            device_id=(to_face, to_tile),
            device_id_type=pl.DeviceIdType.MESH,
        )

    faces = [
        (k, lax.rem(face + k, face_count), lax.rem(face + face_count - k, face_count))
        for k in range(1, face_count)
    ]
    tiles = [
        (k, lax.rem(tile + k, tile_count), lax.rem(tile + tile_count - k, tile_count))
        for k in range(1, tile_count)
    ]

    barrier = pltpu.get_barrier_semaphore()
    for _, to, _ in faces:
        pl.semaphore_signal(
            barrier, inc=1, device_id=(to, tile), device_id_type=pl.DeviceIdType.MESH
        )
    for _, to, _ in tiles:
        pl.semaphore_signal(
            barrier, inc=1, device_id=(face, to), device_id_type=pl.DeviceIdType.MESH
        )
    pl.semaphore_wait(barrier, face_count + tile_count - 2)

    def rows_of(index, size):
        return pl.ds(pl.multiple_of(index * size, 8), size)

    sent = []
    for k, to, _ in faces:
        sent.append(
            copy(
                sums_ref.at[rows_of(to, block)],
                face_box.at[face],
                face_send.at[k],
                face_recv.at[face],
                to,
                tile,
            )
        )
        sent.append(
            copy(
                sums_ref.at[pl.ds(channels, 16)],
                face_extra.at[face],
                face_xsend.at[k],
                face_xrecv.at[face],
                to,
                tile,
            )
        )
    up, down = lax.rem(face + face_count - 1, face_count), lax.rem(face + 1, face_count)
    left, right = lax.rem(tile + tile_count - 1, tile_count), lax.rem(tile + 1, tile_count)
    rim_copies = [
        copy(leaving_ref.at[d], rims.at[(d + 2) % 4], rim_send.at[d], rim_recv.at[(d + 2) % 4], *to)
        for d, to in enumerate([(up, tile), (face, right), (down, tile), (face, left)])
    ]
    for one in sent + rim_copies:
        one.start()
    face_box[face] = sums_ref[rows_of(face, block)]
    face_extra[face] = sums_ref[channels : channels + 16]
    for k, to, source in faces:
        copy(
            face_box.at[source], face_box.at[source], face_send.at[k], face_recv.at[source], to, tile
        ).wait_recv()
        copy(
            face_extra.at[source],
            face_extra.at[source],
            face_xsend.at[k],
            face_xrecv.at[source],
            to,
            tile,
        ).wait_recv()
    acc, small = face_box[0], face_extra[0]
    for f in range(1, face_count):
        acc, small = acc + face_box[f], small + face_extra[f]
    part[...] = acc
    extra[...] = small

    for k, to, _ in tiles:

        @pl.when(to < owners)
        def _():
            copy(
                part.at[rows_of(to, piece)],
                tile_box.at[tile],
                tile_send.at[k],
                tile_recv.at[tile],
                face,
                to,
            ).start()

        one = copy(
            extra, tile_extra.at[tile], tile_xsend.at[k], tile_xrecv.at[tile], face, to
        )
        one.start()
        sent.append(one)
    tile_extra[tile] = extra[...]

    @pl.when(tile < owners)
    def _():
        tile_box[tile] = part[rows_of(tile, piece)]
        for k, to, source in tiles:
            copy(
                tile_box.at[source],
                tile_box.at[source],
                tile_send.at[k],
                tile_recv.at[source],
                face,
                to,
            ).wait_recv()
        acc = tile_box[0]
        for t in range(1, tile_count):
            acc = acc + tile_box[t]
        mine = rows_of(face * owners + tile, piece)
        total[mine] = acc
        for k, to, _ in tiles:
            copy(
                total.at[mine], total.at[mine], tile_gsend.at[k], tile_grecv.at[tile], face, to
            ).start()

    for k, to, source in tiles:

        @pl.when(source < owners)
        def _():
            theirs = rows_of(face * owners + source, piece)
            copy(
                total.at[theirs], total.at[theirs], tile_gsend.at[k], tile_grecv.at[source], face, to
            ).wait_recv()

    mine = rows_of(face, block)
    for k, to, _ in faces:
        one = copy(total.at[mine], total.at[mine], face_gsend.at[k], face_grecv.at[face], to, tile)
        one.start()
        sent.append(one)
    for k, to, source in tiles:
        copy(
            tile_extra.at[source],
            tile_extra.at[source],
            tile_xsend.at[k],
            tile_xrecv.at[source],
            face,
            to,
        ).wait_recv()
    small = tile_extra[0]
    for t in range(1, tile_count):
        small = small + tile_extra[t]
    depth_ref[...] = small[:9]
    bias_ref[...] = small[9:10]
    for one in rim_copies:
        one.wait_recv()
    returned_ref[...] = rims[...]
    for k, to, source in faces:
        theirs = rows_of(source, block)
        copy(
            total.at[theirs], total.at[theirs], face_gsend.at[k], face_grecv.at[source], to, tile
        ).wait_recv()
    point_ref[...] = total[...]
    for one in sent + rim_copies:
        one.wait_send()
    for k, to, _ in tiles:

        @pl.when(to < owners)
        def _():
            copy(
                part.at[rows_of(to, piece)],
                tile_box.at[tile],
                tile_send.at[k],
                tile_recv.at[tile],
                face,
                to,
            ).wait_send()

        @pl.when(tile < owners)
        def _():
            own = rows_of(face * owners + tile, piece)
            copy(
                total.at[own], total.at[own], tile_gsend.at[k], tile_grecv.at[tile], face, to
            ).wait_send()


def return_and_sum(leaving, sums):
    face_count, tile_count = lax.axis_size("face"), lax.axis_size("tile")
    channels = sums.shape[1]
    block = channels // face_count
    piece = block // min(tile_count, block // 8)
    vmem = pl.BlockSpec(memory_space=pltpu.VMEM)
    dma = pltpu.SemaphoreType.DMA
    return pl.pallas_call(
        functools.partial(comm_kernel, face_count, tile_count),
        in_specs=[vmem, vmem],
        out_specs=[vmem] * 4,
        out_shape=[
            jax.ShapeDtypeStruct(leaving.shape, BF16),
            jax.ShapeDtypeStruct((channels, channels), F32),
            jax.ShapeDtypeStruct((9, channels), F32),
            jax.ShapeDtypeStruct((1, channels), F32),
        ],
        scratch_shapes=[
            pltpu.VMEM(leaving.shape, BF16),
            pltpu.VMEM((face_count, block, channels), F32),
            pltpu.VMEM((face_count, 16, channels), F32),
            pltpu.VMEM((tile_count, piece, channels), F32),
            pltpu.VMEM((tile_count, 16, channels), F32),
            pltpu.VMEM((block, channels), F32),
            pltpu.VMEM((16, channels), F32),
            pltpu.VMEM((channels, channels), F32),
            dma((4,)),
            dma((4,)),
        ]
        + [dma((face_count,))] * 4
        + [dma((tile_count,))] * 6
        + [dma((face_count,))] * 2,
        compiler_params=pltpu.CompilerParams(
            collective_id=0, has_side_effects=True, vmem_limit_bytes=32 * 2**20
        ),
    )(leaving, sums)


def shards(
    state_field,
    cotangent,
    depth_weight,
    depth_bias,
    point_weight,
    tile_links,
    link_sides,
    link_flips,
    corner_masks,
):
    batch, side, _, channels = state_field.shape
    face_count = lax.axis_size("face")
    tile_count = lax.axis_size("tile")
    face_pos = lax.axis_index("face")
    tile_pos = lax.axis_index("tile")
    toward = jnp.stack(
        [
            (face_pos - 1) % face_count * tile_count + tile_pos,
            face_pos * tile_count + (tile_pos + 1) % tile_count,
            (face_pos + 1) % face_count * tile_count + tile_pos,
            face_pos * tile_count + (tile_pos - 1) % tile_count,
        ]
    )
    matched = tile_links[0][:, None] == toward[None, :]
    counter = jnp.arange(4, dtype=jnp.int32)
    dir_of_side = jnp.sum(jnp.where(matched, counter[None, :], 0), axis=1)
    side_of_dir = jnp.sum(jnp.where(matched, counter[:, None], 0), axis=0)
    norm_scale = float(batch * side * side * face_count * tile_count) ** (-0.5)

    edges = jnp.stack(
        [state_field[:, 0], state_field[:, :, -1], state_field[:, -1], state_field[:, :, 0]]
    )
    rims = exchange(jnp.take(edges, side_of_dir, axis=0))
    links = jnp.stack([dir_of_side, link_flips[0], corner_masks[0]])

    whole = pl.BlockSpec((1, side, side, channels), lambda b, s: (b, 0, 0, 0))
    rows_of = pl.BlockSpec((1, ROWS, side, channels), lambda b, s: (b, s, 0, 0))
    fixed = lambda *shape: pl.BlockSpec(shape, lambda b, s: (0,) * len(shape))
    pixels = batch * side * side
    sum_rows = channels + 16
    grad_hidden, leaving, sums = pl.pallas_call(
        functools.partial(first_kernel, norm_scale),
        grid=(batch, side // ROWS),
        in_specs=[
            whole,
            rows_of,
            pl.BlockSpec((4, 1, side, channels), lambda b, s: (0, b, 0, 0)),
            pl.BlockSpec(memory_space=pltpu.SMEM),
            fixed(9, channels),
            fixed(1, channels),
            fixed(channels, channels),
        ],
        out_specs=[
            rows_of,
            pl.BlockSpec((4, 1, side, channels), lambda b, s: (0, b, 0, 0)),
            fixed(sum_rows, channels),
        ],
        out_shape=[
            jax.ShapeDtypeStruct(state_field.shape, BF16),
            jax.ShapeDtypeStruct((4, batch, side, channels), BF16),
            jax.ShapeDtypeStruct((sum_rows, channels), F32),
        ],
        scratch_shapes=[
            pltpu.VMEM((3, side + 2, side, channels), F32),
            pltpu.VMEM((ROWS, side, channels), F32),
            pltpu.VMEM((ROWS, side, channels), BF16),
            pltpu.VMEM((10, 8, channels), F32),
        ]
        + [pltpu.VMEM((side, 1, channels), F32)] * 4
        + [pltpu.VMEM((4, side, channels), F32)],
        compiler_params=pltpu.CompilerParams(vmem_limit_bytes=48 * 2**20),
        cost_estimate=pl.CostEstimate(
            flops=4 * pixels * channels * channels,
            bytes_accessed=6 * pixels * channels,
            transcendentals=pixels * channels,
        ),
    )(
        state_field,
        cotangent,
        rims,
        links,
        depth_weight,
        depth_bias[None],
        point_weight,
    )

    returned, point_sum, depth_sum, bias_sum = return_and_sum(
        leaving.reshape(4, batch * side, channels), sums
    )

    whole = pl.BlockSpec((1, side, side, channels), lambda b: (b, 0, 0, 0))
    field_grad = pl.pallas_call(
        second_kernel,
        grid=(batch,),
        in_specs=[
            whole,
            pl.BlockSpec((4, 1, side, channels), lambda b: (0, b, 0, 0)),
            pl.BlockSpec(memory_space=pltpu.SMEM),
            pl.BlockSpec((9, channels), lambda b: (0, 0)),
        ],
        out_specs=whole,
        scratch_shapes=[
            pltpu.VMEM((side, channels), F32),
            pltpu.VMEM((side, channels), F32),
            pltpu.VMEM((side, 1, channels), F32),
            pltpu.VMEM((side, 1, channels), F32),
        ],
        out_shape=jax.ShapeDtypeStruct(state_field.shape, BF16),
        compiler_params=pltpu.CompilerParams(vmem_limit_bytes=48 * 2**20),
        cost_estimate=pl.CostEstimate(
            flops=40 * pixels * channels,
            bytes_accessed=4 * pixels * channels,
            transcendentals=0,
        ),
    )(
        grad_hidden,
        returned.reshape(leaving.shape),
        links,
        depth_weight,
    )
    return field_grad, depth_sum, bias_sum[0], point_sum


def solution(mesh):
    in_specs = (
        P(None, "face", "tile", None),
        P(None, "face", "tile", None),
        P(),
        P(),
        P(),
        P(("face", "tile"), None),
        P(("face", "tile"), None),
        P(("face", "tile"), None),
        P(("face", "tile"), None),
    )
    out_specs = (P(None, "face", "tile", None), P(), P(), P())
    return jax.shard_map(shards, mesh=mesh, in_specs=in_specs, out_specs=out_specs, check_vma=False)
```
